512 devices in a mesh: wide: 32 (over y, z_lo), blk: 16 (over x, z_hi, core).
Axes of the slice: x: 4, y: 4, z: 16 (z_hi: 2, z_lo: 8; z = z_hi * 8 + z_lo), core: 2. Of those that a mesh axis runs over, the one named last changes fastest.
Arguments:
- source_strength: bfloat16 [16, 128, 128, 256], P('blk', 'wide'), may hold values from -0.75 to 0.75
- adjoint_strength: bfloat16 [16, 128, 128, 256], P('blk', 'wide'), may hold values from -0.75 to 0.75
- node_points: bfloat16 [16, 128, 3, 128], P('blk', 'wide'), may hold values from -2 to 2
- near_rows: int32 [16, 128, 32], P('blk', 'wide'), may hold values from 0 to 127, as said below
- counts_rows: int32 [16, 128], P('blk', 'wide'), may hold values from 1 to 32
- near_cols: int32 [16, 128, 16], P('blk', 'wide'), may hold values from 0 to 63, as said below
- counts_cols: int32 [16, 128], P('blk', 'wide'), may hold values from 1 to 16
Outputs:
- shape_gradient: float32 [16, 128, 3, 128], P('blk', 'wide')
The draws below stay inside these ranges and needn't reach their ends.
Inputs may be any that keep to these rules, and one draw needn't show every extreme that they name: `near_rows`: for each block, its first counts_rows entries are distinct and ascending; the entries after them are unused. `near_cols`: for each block, its first counts_cols entries are distinct and ascending; the entries after them are unused.
All inputs are finite; a program needn't handle non-finite values.
Results may differ from the reference program's by a relative error of at most 0.0003.
Values may be sent and summed in bfloat16 or wider, within the bound.
A program may use at most 64 MiB of HBM per device.

```python
import jax
import jax.numpy as jnp
from jax import lax

K = 256
BLK = 128
BLK_DEV = 4
PANELS = 16
PANEL_BLOCKS = 128
COL_BLOCKS = 64
NEAR_A = 32
NEAR_B = 16
N_WIDE = 32


def near_pattern(key, salt, candidates, listed):
    key = jax.random.fold_in(key, salt)
    keys = jax.random.split(key, 5)
    devices_panel = PANEL_BLOCKS // BLK_DEV
    heavy = jax.random.randint(keys[0], (PANELS, devices_panel, 1), 0, 8) == 0
    heavy = jnp.repeat(heavy, BLK_DEV, axis=2).reshape(PANELS, PANEL_BLOCKS)
    light_top = max(1, listed // 4) + 1
    light = jax.random.randint(keys[1], (PANELS, PANEL_BLOCKS), 1, light_top)
    heavy_low = max(1, 3 * listed // 4)
    loaded = jax.random.randint(keys[2], (PANELS, PANEL_BLOCKS), heavy_low, listed + 1)
    counts = jnp.where(heavy, loaded, light).reshape(PANELS * PANEL_BLOCKS)
    chosen_spot = jax.random.randint(keys[3], (), 0, PANELS * PANEL_BLOCKS)
    counts = jnp.where(jnp.arange(PANELS * PANEL_BLOCKS) == chosen_spot, listed, counts)
    counts = counts.reshape(PANELS, PANEL_BLOCKS).astype(jnp.int32)
    scores = jax.random.randint(keys[4], (PANELS, PANEL_BLOCKS, candidates), 0, 1 << 20) * candidates
    scores = scores + jnp.arange(candidates, dtype=jnp.int32)
    ranks = jnp.argsort(jnp.argsort(scores, axis=-1), axis=-1)
    picked = ranks < counts[:, :, None]
    ordering = jnp.where(picked, 0, candidates) + jnp.arange(candidates, dtype=jnp.int32)
    lists = jnp.argsort(ordering, axis=-1)[:, :, :listed].astype(jnp.int32)
    return (lists, counts)


def draw_near_rows(key, part):
    return near_pattern(key, 11, PANEL_BLOCKS, NEAR_A)[0]


def draw_counts_rows(key, part):
    return near_pattern(key, 11, PANEL_BLOCKS, NEAR_A)[1]


def draw_near_cols(key, part):
    return near_pattern(key, 23, COL_BLOCKS, NEAR_B)[0]


def draw_counts_cols(key, part):
    return near_pattern(key, 23, COL_BLOCKS, NEAR_B)[1]


def levels(own_key, dims, cuts, low, top_value):
    def one(dim, blocks):
        draws = jax.random.uniform(jax.random.fold_in(jax.random.fold_in(own_key, 6), dim), (blocks,), jnp.float32, low / len(cuts), top_value / len(cuts))
        return jnp.repeat(jnp.exp(draws), dims[dim] // blocks).reshape((-1,) + (1,) * (len(dims) - dim - 1))

    gain = one(*cuts[0])
    for cut in cuts[1:]:
        gain = gain * one(*cut)
    return gain


def centred(rng, dims, spread, bound, cuts=(), held_as=jnp.bfloat16):
    entries = jax.random.normal(rng, dims, jnp.float32) * spread
    if len(cuts) > 0:
        entries = levels(rng, dims, cuts, -0.22, 0.18) * entries
    return jnp.clip(entries, min=-bound, max=bound).astype(held_as)


def setup_inputs(seed: int = 0) -> dict:
    key_list = jax.random.split(jax.random.key(seed), 8)
    return {
        "source_strength": centred(key_list[0], (PANELS, PANEL_BLOCKS, BLK, K), 0.125, 0.75, ((0, 16), (1, 32))),
        "adjoint_strength": centred(key_list[1], (PANELS, PANEL_BLOCKS, BLK, K), 0.125, 0.75, ((0, 16), (1, 32))),
        "node_points": jnp.clip(jax.random.uniform(key_list[2], (PANELS, PANEL_BLOCKS, 3, BLK), jnp.float32, -2.0, 2.0) * levels(key_list[2], (PANELS, PANEL_BLOCKS, 3, BLK), ((0, 16), (1, 32)), -0.4, 0.0), -2.0, 2.0).astype(jnp.bfloat16),
        "near_rows": draw_near_rows(jax.random.fold_in(key_list[7], 71), 0),
        "counts_rows": draw_counts_rows(jax.random.fold_in(key_list[7], 71), 0),
        "near_cols": draw_near_cols(jax.random.fold_in(key_list[7], 71), 0),
        "counts_cols": draw_counts_cols(jax.random.fold_in(key_list[7], 71), 0),
    }


EPS2 = 0.04

def pair_sum(own_points, own_values, far_points, far_values, partner_lists, counts, lowest, extent, per_turn):
    blocks, listed = partner_lists.shape
    all_slots = blocks * listed
    partner = partner_lists.reshape(all_slots).astype(jnp.int32)
    owners = lax.broadcasted_iota(jnp.int32, (blocks, listed), 0).reshape(all_slots)
    active = (lax.broadcasted_iota(jnp.int32, (blocks, listed), 1) < counts[:, None]).reshape(all_slots)
    active = active & (partner >= lowest) & (partner < lowest + extent)
    ranking = jnp.argsort(jnp.where(active, 0, all_slots).astype(jnp.int32) + jnp.arange(all_slots, dtype=jnp.int32))
    live_count = jnp.sum(active.astype(jnp.int32))
    own_index = jnp.pad(owners[ranking], (0, per_turn))
    far_index = jnp.pad(jnp.clip(partner[ranking] - lowest, 0, extent - 1), (0, per_turn))
    size_block = own_points.shape[-1]

    def step(step_index, running):
        offset = (step_index * per_turn).astype(jnp.int32)
        own_batch = lax.dynamic_slice_in_dim(own_index, offset, per_turn)
        far_batch = lax.dynamic_slice_in_dim(far_index, offset, per_turn)
        valid = (offset + jnp.arange(per_turn, dtype=jnp.int32) < live_count).astype(jnp.float32)
        left = own_values[own_batch].astype(jnp.float32)
        right = far_values[far_batch].astype(jnp.float32)
        weights = jnp.einsum('gik,gjk->gij', left, right)
        own_batch_points = own_points[own_batch].astype(jnp.float32)
        far_batch_points = far_points[far_batch].astype(jnp.float32)
        separation = far_batch_points[:, :, None, :] - own_batch_points[:, :, :, None]
        distance = lax.optimization_barrier(jnp.sum(separation * separation, axis=1)) + EPS2
        inverse = lax.rsqrt(distance)
        scaled = weights * (inverse * inverse * inverse) * valid[:, None, None]
        contrib = lax.optimization_barrier(jnp.sum(separation * scaled[:, None, :, :], axis=3))
        return running.at[own_batch].add(contrib)
    turns = (live_count + per_turn - 1) // per_turn
    return lax.fori_loop(0, turns, step, jnp.zeros((blocks, 3, size_block), jnp.float32))

def reference(source_strength, adjoint_strength, node_points, near_rows, counts_rows, near_cols, counts_cols):

    def panel_term(panel):
        return pair_sum(node_points[panel], adjoint_strength[panel], node_points[panel], source_strength[panel], near_rows[panel], counts_rows[panel], 0, PANEL_BLOCKS, 8)
    grad_rows = lax.map(panel_term, jnp.arange(PANELS, dtype=jnp.int32))

    def column_term(column):
        start = (column * BLK_DEV).astype(jnp.int32)
        points = lax.dynamic_slice_in_dim(node_points, start, BLK_DEV, 1).reshape(COL_BLOCKS, 3, BLK)
        sources = lax.dynamic_slice_in_dim(source_strength, start, BLK_DEV, 1).reshape(COL_BLOCKS, BLK, K)
        adjoints = lax.dynamic_slice_in_dim(adjoint_strength, start, BLK_DEV, 1).reshape(COL_BLOCKS, BLK, K)
        lists = lax.dynamic_slice_in_dim(near_cols, start, BLK_DEV, 1).reshape(COL_BLOCKS, NEAR_B)
        counts = lax.dynamic_slice_in_dim(counts_cols, start, BLK_DEV, 1).reshape(COL_BLOCKS)
        result = pair_sum(points, sources, points, adjoints, lists, counts, 0, COL_BLOCKS, 8)
        return result.reshape(PANELS, BLK_DEV, 3, BLK)
    grad_cols = lax.map(column_term, jnp.arange(N_WIDE, dtype=jnp.int32))
    grad_cols = jnp.transpose(grad_cols, (1, 0, 2, 3, 4)).reshape(PANELS, PANEL_BLOCKS, 3, BLK)
    return grad_rows + grad_cols
```

```python
import functools

import jax
import jax.numpy as jnp
from jax import lax
from jax.experimental import pallas as pl
from jax.experimental.pallas import tpu as pltpu
from jax.sharding import PartitionSpec as P

EPS2 = 0.04
MESH = pl.DeviceIdType.MESH
F32 = jnp.float32

NZ = 8
HALF = NZ // 2
AHEAD = NZ
SIBLING = AHEAD + HALF
SOURCES_Y = SIBLING + 2
MAX_PAIRS_ROWS = 6


class Place:
    def __init__(self, nx, ny):
        self.nx, self.ny = nx, ny
        self.wide, self.blk = lax.axis_index("wide"), lax.axis_index("blk")
        self.y, self.z = self.wide // NZ, self.wide % NZ
        self.x, self.h, self.c = self.blk // 4, (self.blk // 2) % 2, self.blk % 2

    def at(self, y=None, z=None, x=None, h=None, c=None):
        pick = lambda given, mine: mine if given is None else given
        wide = pick(y, self.y) * NZ + pick(z, self.z)
        blk = pick(x, self.x) * 4 + pick(h, self.h) * 2 + pick(c, self.c)
        return {"wide": wide, "blk": blk}

    def beside(self, right):
        if right:
            crosses = (self.z == NZ - 1).astype(jnp.int32)
            z = (self.z + 1) % NZ
        else:
            crosses = (self.z == 0).astype(jnp.int32)
            z = (self.z + NZ - 1) % NZ
        return self.at(z=z, h=(self.h + crosses) % 2)

    def others_z(self):
        return [((self.z + d) % NZ, self.at(z=(self.z + d) % NZ)) for d in range(1, NZ)]

    def others_y(self):
        return [self.at(y=(self.y + d) % self.ny) for d in range(1, self.ny)]

    def others_x(self):
        return [((self.x + d) % self.nx, self.at(x=(self.x + d) % self.nx)) for d in range(1, self.nx)]

    def others_hc(self):
        return [self.at(h=(self.h + rel // 2) % 2, c=(self.c + rel % 2) % 2) for rel in (1, 2, 3)]


def greet(devices):
    barrier = pltpu.get_barrier_semaphore()
    for device in devices:
        pl.semaphore_signal(barrier, inc=1, device_id=device, device_id_type=MESH)


def await_greetings(count):
    pl.semaphore_wait(pltpu.get_barrier_semaphore(), count)


def near_mask(near, counts, width):
    blocks, listed = near.shape
    lanes = lax.broadcasted_iota(jnp.int32, (blocks, width), 1)
    mask = jnp.zeros((blocks, width), F32)
    for n in range(listed):
        hit = jnp.where(near[:, n : n + 1] == lanes, 1.0, 0.0)
        mask = mask + jnp.where(counts > n, hit, 0.0)
    return mask


def pair_list(place, row_mask, col_mask):
    z, h, c, x, ny = place.z, place.h, place.c, place.x, place.ny
    sources_x = SOURCES_Y + ny
    rows, cols = row_mask.shape[0], col_mask.shape[0]
    own = rows + cols
    lane = lax.broadcasted_iota(jnp.int32, (128, 128), 0)
    k = lax.broadcasted_iota(jnp.int32, (128, 128), 1)
    rel = k // 4
    from_row = (k // 4) * (NZ * 4) + z * 4 + k % 4
    from_col = x * 16 + ((rel // 2 + h) % 2) * 8 + ((rel + c) % 2) * 4 + k % 4
    bf = jnp.bfloat16
    pick_row = jnp.where((lane == from_row) & (k < ny * 4), 1.0, 0.0).astype(bf)
    pick_col = jnp.where((lane == from_col) & (k < 16), 1.0, 0.0).astype(bf)
    dot = functools.partial(jnp.dot, preferred_element_type=F32)
    live = jnp.concatenate([dot(row_mask.astype(bf), pick_row), dot(col_mask.astype(bf), pick_col)], axis=0)
    before = dot(live.astype(bf), jnp.where(lane < k, 1.0, 0.0).astype(bf))
    totals = jnp.broadcast_to(jnp.sum(live, axis=1, keepdims=True), (own, 128))
    above = lax.broadcasted_iota(jnp.int32, (own, own), 0) > lax.broadcasted_iota(jnp.int32, (own, own), 1)
    offset = dot(jnp.where(above, 1.0, 0.0).astype(bf), totals.astype(bf))
    rank = jnp.where(live > 0.5, before + offset, -1.0)

    a = lax.broadcasted_iota(jnp.int32, (own, 128), 0)
    k = lax.broadcasted_iota(jnp.int32, (own, 128), 1)
    rel = k // 4
    unit = jnp.where(
        rel == 0, z, jnp.where(rel == 1, SIBLING, jnp.where(rel == 2, AHEAD + z % HALF, SIBLING + 1))
    )
    is_row = a < rows
    own_block = jnp.where(is_row, a, a - rows + sources_x * 4)
    far_block = jnp.where(is_row, SOURCES_Y * 4 + k, unit * 4 + k % 4)
    far_slot = jnp.where(is_row, k, ny * 4 + k)
    code = (own_block + 128 * far_block + 16384 * far_slot).astype(F32)

    fill = jnp.zeros((128 - own, 128), F32)
    rank_t = jnp.transpose(jnp.concatenate([rank, fill - 1.0], axis=0))[:16]
    code_t = jnp.transpose(jnp.concatenate([code, fill], axis=0))[:16]
    slots = lax.broadcasted_iota(jnp.int32, (16, 128), 1).astype(F32)
    packed = [jnp.zeros((16, 128), F32) for _ in range(MAX_PAIRS_ROWS)]
    for one in range(own):
        rank_one = jnp.broadcast_to(rank_t[:, one : one + 1], (16, 128))
        code_one = jnp.broadcast_to(code_t[:, one : one + 1], (16, 128))
        for r in range(MAX_PAIRS_ROWS):
            packed[r] = packed[r] + jnp.where(rank_one == slots + 128.0 * r, code_one, 0.0)
    listing = [jnp.sum(part, axis=0, keepdims=True) for part in packed]
    count = jnp.broadcast_to(jnp.sum(jnp.sum(live, axis=1, keepdims=True), axis=0, keepdims=True), (2, 128))
    return jnp.concatenate(listing + [count], axis=0).astype(jnp.int32)


def gather_kernel(
    nx,
    ny,
    source_ref,
    adjoint_ref,
    points_ref,
    near_rows_ref,
    counts_rows_ref,
    near_cols_ref,
    counts_cols_ref,
    blocks_ref,
    meta_ref,
    list_ref,
    own_meta,
    ring_send,
    ring_recv,
    core_send,
    core_recv,
    y_send,
    y_recv,
    x_send,
    x_recv,
    meta_send,
    meta_recv,
    local_sem,
):
    place = Place(nx, ny)
    z, x, y = place.z, place.x, place.y
    per_device = source_ref.shape[0]
    sources_x = SOURCES_Y + ny
    right, left = place.beside(True), place.beside(False)
    sides = (right, left)
    others_z, others_y, others_x, others_hc = (
        place.others_z(),
        place.others_y(),
        place.others_x(),
        place.others_hc(),
    )
    sibling = others_hc[0]
    met = [device for _, device in others_z] + others_y + [device for _, device in others_x] + others_hc
    met = met + [right, left]
    greet(met)

    own_meta[...] = jnp.zeros_like(own_meta)
    row_mask = near_mask(near_rows_ref[...], counts_rows_ref[...], 128)
    col_mask = near_mask(near_cols_ref[...], counts_cols_ref[...], 128)
    for b in range(per_device):
        own_meta[b, 0:3, :] = points_ref[b].astype(F32)
        own_meta[b, 4:5, :] = row_mask[b : b + 1]
        own_meta[b, 5:6, :] = col_mask[b : b + 1]

    await_greetings(len(met))

    def remote(src, dst, send, recv, device):
        return pltpu.make_async_remote_copy(
            src_ref=src, dst_ref=dst, send_sem=send, recv_sem=recv, device_id=device, device_id_type=MESH
        )

    def mirrored(side):
        return z if side == 0 else NZ - 1 - z

    def unit_of(side, m, t):
        near = m - 1 - t
        ahead = 3 - (t - m)
        if side == 0:
            return jnp.where(t < m, near, AHEAD + ahead)
        return jnp.where(t < m, NZ - 1 - near, AHEAD + 3 - ahead)

    def arrivals(m):
        return jnp.where(m < HALF, HALF, m)

    def forwards(m, t):
        last = m == NZ - 1
        return jnp.where(m < HALF, t < HALF - 1, jnp.where(last, t >= HALF - 1, True)) & (t < arrivals(m))

    def sent_unit(side, m, unit):
        crossed = AHEAD + unit if side == 0 else AHEAD + unit - HALF
        return jnp.where(m == NZ - 1, crossed, unit)

    def sent_number(m, t):
        return jnp.where(m == NZ - 1, t - (HALF - 1), t + 1)

    def ring_copy(side, t, b):
        m = mirrored(side)
        unit = unit_of(side, m, t)
        return remote(
            blocks_ref.at[unit, b],
            blocks_ref.at[sent_unit(side, m, unit), b],
            ring_send.at[side, t + 1, b],
            ring_recv.at[side, sent_number(m, t), b],
            sides[side],
        )

    def own_copy(side, b):
        return remote(
            adjoint_ref.at[b],
            blocks_ref.at[z, b],
            ring_send.at[side, 0, b],
            ring_recv.at[side, 0, b],
            sides[side],
        )

    def arrival(side, t, b):
        unit = unit_of(side, mirrored(side), t)
        slot = blocks_ref.at[unit, b]
        return remote(slot, slot, ring_send.at[side, t + 1, b], ring_recv.at[side, t, b], sides[side])

    def core_copy(b):
        return remote(
            blocks_ref.at[AHEAD + z % HALF, b],
            blocks_ref.at[SIBLING + 1, b],
            core_send.at[b],
            core_recv.at[b],
            sibling,
        )

    core_own = remote(
        adjoint_ref, blocks_ref.at[SIBLING], core_send.at[per_device], core_recv.at[per_device], sibling
    )

    for b in range(per_device):
        for side in (0, 1):

            @pl.when(mirrored(side) < NZ - 1)
            def _():
                own_copy(side, b).start()

    metas = []
    own_slots = [z, NZ + x, NZ + nx + y, NZ + nx + ny]
    for d, (_, device) in enumerate(others_z):
        metas.append((own_slots[0], d, device, (z + NZ - 1 - d) % NZ))
    for d, (_, device) in enumerate(others_x):
        metas.append((own_slots[1], NZ + d, device, NZ + (x + nx - 1 - d) % nx))
    for d, device in enumerate(others_y):
        metas.append((own_slots[2], NZ + nx + d, device, NZ + nx + (y + ny - 1 - d) % ny))
    for d, device in enumerate(others_hc):
        metas.append((NZ + nx + ny + 1 + d, NZ + nx + ny + d, device, NZ + nx + ny + 1 + d))
    meta_out = [
        remote(own_meta, meta_ref.at[slot], meta_send.at[s], meta_recv.at[s], device)
        for slot, s, device, _ in metas
    ]
    meta_in = [
        remote(own_meta, meta_ref.at[slot], meta_send.at[s], meta_recv.at[s], device)
        for _, s, device, slot in metas
    ]
    for copy in meta_out:
        copy.start()
    core_own.start()
    y_out, y_in, x_out, x_in = [], [], [], []
    for d, device in enumerate(others_y):
        sems = (y_send.at[d], y_recv.at[d], device)
        y_out.append(remote(source_ref, blocks_ref.at[SOURCES_Y + y], *sems))
        y_in.append(remote(source_ref, blocks_ref.at[SOURCES_Y + (y + ny - 1 - d) % ny], *sems))
    for d, (_, device) in enumerate(others_x):
        sems = (x_send.at[d], x_recv.at[d], device)
        x_out.append(remote(source_ref, blocks_ref.at[sources_x + x], *sems))
        x_in.append(remote(source_ref, blocks_ref.at[sources_x + (x + nx - 1 - d) % nx], *sems))
    for copy in y_out + x_out:
        copy.start()
    locals_ = [
        pltpu.make_async_copy(adjoint_ref, blocks_ref.at[z], local_sem.at[0]),
        pltpu.make_async_copy(source_ref, blocks_ref.at[SOURCES_Y + y], local_sem.at[1]),
        pltpu.make_async_copy(source_ref, blocks_ref.at[sources_x + x], local_sem.at[2]),
    ]
    for copy in locals_:
        copy.start()
    for slot in own_slots:
        meta_ref[slot] = own_meta[...]

    def due(m, hops):
        near = hops < m
        ahead = (m < HALF) & (hops >= HALF + m) & (hops < 2 * HALF)
        return near | ahead, jnp.where(near, hops, hops - HALF)

    def ring_step(s, carry):
        hops, b = s // per_device, s % per_device
        for side in (0, 1):
            m = mirrored(side)
            comes, t = due(m, hops)

            @pl.when(comes)
            def _():
                arrival(side, t, b).wait_recv()

                @pl.when(forwards(m, t))
                def _():
                    ring_copy(side, t, b).start()

                @pl.when((m < HALF) & (t == HALF - 1))
                def _():
                    core_copy(b).start()

        return carry

    lax.fori_loop(0, 2 * per_device, ring_step, 0)

    for copy in meta_in:
        copy.wait_recv()
    tiles = NZ * per_device
    row_masks = jnp.concatenate([meta_ref[u, b, 4:5, :] for u in range(NZ) for b in range(per_device)], axis=0)
    col_masks = jnp.concatenate(
        [meta_ref[NZ + u, b, 5:6, :] for u in range(nx) for b in range(per_device)], axis=0
    )
    list_ref[...] = pair_list(place, row_masks, col_masks)

    lax.fori_loop(2 * per_device, NZ * per_device, ring_step, 0)

    for copy in y_in + x_in:
        copy.wait_recv()
    for b in range(per_device):
        core_copy(b).wait_recv()
    core_own.wait_recv()
    for copy in locals_:
        copy.wait()
    for copy in y_out + x_out + meta_out + [core_own]:
        copy.wait_send()
    for b in range(per_device):
        core_copy(b).wait_send()
        for side in (0, 1):

            @pl.when(mirrored(side) < NZ - 1)
            def _():
                own_copy(side, b).wait_send()

    def sent_step(s, carry):
        t, b = s // per_device, s % per_device
        for side in (0, 1):

            @pl.when(forwards(mirrored(side), t))
            def _():
                ring_copy(side, t, b).wait_send()

        return carry

    lax.fori_loop(0, (NZ - 1) * per_device, sent_step, 0)


UNROLL = 4


def pair_kernel(rows, own, shift, list_ref, blocks_hbm, meta_ref, out_ref, blocks, far_axes, acc, sems):
    units, per_device = blocks_hbm.shape[:2]
    copies = [
        pltpu.make_async_copy(blocks_hbm.at[u], blocks.at[pl.ds(u * per_device, per_device)], sems.at[u])
        for u in range(units)
    ]
    for copy in copies:
        copy.start()
    acc[...] = jnp.zeros_like(acc)
    fars = far_axes.shape[0]
    axis = lax.broadcasted_iota(jnp.int32, (8, 3 * 128), 0)
    wanted = lax.broadcasted_iota(jnp.int32, (8, 3 * 128), 1) // 128
    spread = jnp.where(axis == wanted, 1.0, 0.0)

    def spread_far(j, carry):
        tile = meta_ref[own + j]
        far_axes[j] = lax.dot_general(
            tile, spread, (((0,), (0,)), ((), ())), preferred_element_type=F32, precision=lax.Precision.HIGHEST
        )
        return carry

    lax.fori_loop(0, fars, spread_far, 0)
    for copy in copies:
        copy.wait()
    count = list_ref[MAX_PAIRS_ROWS, 0]

    def one_pair(k):
        code = list_ref[k // 128, k % 128]
        own_block, far_block, far_slot = code & 127, (code >> 7) & 127, code >> 14
        acc_slot = jnp.where(own_block < rows, own_block, own_block - shift)
        weights = lax.dot_general(
            blocks[far_block], blocks[own_block], (((1,), (1,)), ((), ())), preferred_element_type=F32
        )
        tile = meta_ref[acc_slot]
        own_axes = [jnp.broadcast_to(tile[c : c + 1], (8, 128)) for c in range(3)]
        sums = [jnp.zeros((8, 128), F32) for _ in range(3)]
        for r in range(16):
            at = slice(8 * r, 8 * r + 8)
            d = [far_axes[far_slot, at, 128 * c : 128 * c + 128] - own_axes[c] for c in range(3)]
            inverse = lax.rsqrt(d[0] * d[0] + d[1] * d[1] + d[2] * d[2] + EPS2)
            scaled = weights[at] * (inverse * inverse * inverse)
            sums = [sums[c] + d[c] * scaled for c in range(3)]
        return jnp.where(k < count, acc_slot, own), sums

    def step(i, carry):
        done = [one_pair(i * UNROLL + u) for u in range(UNROLL)]
        for slot, sums in done:
            for c in range(3):
                acc[slot, c] = acc[slot, c] + sums[c]
        return carry

    lax.fori_loop(0, (count + UNROLL - 1) // UNROLL, step, 0)
    out_ref[...] = jnp.zeros_like(out_ref)
    for a in range(own):
        for c in range(3):
            out_ref[a // per_device, (a % per_device) * 4 + c : (a % per_device) * 4 + c + 1, :] = jnp.sum(
                acc[a, c], axis=0, keepdims=True
            )


def return_kernel(nx, ny, parts_ref, out_ref, landed, send_sem, recv_sem):
    place = Place(nx, ny)
    z, x = place.z, place.x
    others_z, others_x = place.others_z(), place.others_x()
    met = [device for _, device in others_z] + [device for _, device in others_x]
    greet(met)
    landed[z] = parts_ref[z]
    landed[NZ + x] = parts_ref[NZ + x]
    await_greetings(len(met))
    outgoing, incoming = [], []

    def both(s, theirs, mine, source, device):
        for slot, copies in ((mine, outgoing), (source, incoming)):
            copies.append(
                pltpu.make_async_remote_copy(
                    src_ref=parts_ref.at[theirs],
                    dst_ref=landed.at[slot],
                    send_sem=send_sem.at[s],
                    recv_sem=recv_sem.at[s],
                    device_id=device,
                    device_id_type=MESH,
                )
            )

    for d, (other, device) in enumerate(others_z):
        both(d, other, z, (z + NZ - 1 - d) % NZ, device)
    for d, (other, device) in enumerate(others_x):
        both(NZ + d, NZ + other, NZ + x, NZ + (x + nx - 1 - d) % nx, device)
    for copy in outgoing:
        copy.start()
    for copy in incoming:
        copy.wait_recv()
    total = landed[0]
    for u in range(1, NZ + nx):
        total = total + landed[u]
    for b in range(out_ref.shape[0]):
        out_ref[b] = total[4 * b : 4 * b + 3]
    for copy in outgoing:
        copy.wait_send()


def shards(
    nx,
    ny,
    source_strength,
    adjoint_strength,
    node_points,
    near_rows,
    counts_rows,
    near_cols,
    counts_cols,
):
    _, per_device, size_block, conditions = source_strength.shape
    units = SOURCES_Y + ny + nx
    metas = NZ + nx + ny + 4
    dma = pltpu.SemaphoreType.DMA
    any_space = pl.BlockSpec(memory_space=pl.ANY)
    vmem = pl.BlockSpec(memory_space=pltpu.VMEM)
    blocks, meta, listing = pl.pallas_call(
        functools.partial(gather_kernel, nx, ny),
        name="gather",
        out_shape=(
            jax.ShapeDtypeStruct((units, per_device, size_block, conditions), jnp.bfloat16),
            jax.ShapeDtypeStruct((metas, per_device, 8, 128), F32),
            jax.ShapeDtypeStruct((8, 128), jnp.int32),
        ),
        in_specs=[any_space, any_space] + [vmem] * 5,
        out_specs=(any_space, vmem, vmem),
        scratch_shapes=[
            pltpu.VMEM((per_device, 8, 128), F32),
            dma((2, NZ, per_device)),
            dma((2, NZ, per_device)),
            dma((per_device + 1,)),
            dma((per_device + 1,)),
            dma((max(ny - 1, 1),)),
            dma((max(ny - 1, 1),)),
            dma((max(nx - 1, 1),)),
            dma((max(nx - 1, 1),)),
            dma((metas,)),
            dma((metas,)),
            dma((3,)),
        ],
        compiler_params=pltpu.CompilerParams(
            collective_id=0, has_side_effects=True, vmem_limit_bytes=16 * 1024 * 1024
        ),
    )(
        source_strength[0],
        adjoint_strength[0],
        node_points[0],
        near_rows[0],
        counts_rows[0][:, None],
        near_cols[0],
        counts_cols[0][:, None],
    )
    rows = NZ * per_device
    own = rows + nx * per_device
    fars = (ny + 4) * per_device
    shift = (SOURCES_Y + ny) * per_device - rows
    parts = pl.pallas_call(
        functools.partial(pair_kernel, rows, own, shift),
        name="pairs",
        out_shape=jax.ShapeDtypeStruct((NZ + nx, 4 * per_device, 128), F32),
        in_specs=[pl.BlockSpec(memory_space=pltpu.SMEM), any_space, vmem],
        out_specs=vmem,
        scratch_shapes=[
            pltpu.VMEM((units * per_device, size_block, conditions), jnp.bfloat16),
            pltpu.VMEM((fars, 128, 3 * 128), F32),
            pltpu.VMEM((own + 1, 3, 8, 128), F32),
            dma((units,)),
        ],
        compiler_params=pltpu.CompilerParams(vmem_limit_bytes=32 * 1024 * 1024),
    )(listing, blocks, meta.reshape(metas * per_device, 8, 128))
    total = pl.pallas_call(
        functools.partial(return_kernel, nx, ny),
        name="sums",
        out_shape=jax.ShapeDtypeStruct((per_device, 3, 128), F32),
        in_specs=[vmem],
        out_specs=vmem,
        scratch_shapes=[
            pltpu.VMEM((NZ + nx, 4 * per_device, 128), F32),
            dma((NZ + nx,)),
            dma((NZ + nx,)),
        ],
        compiler_params=pltpu.CompilerParams(collective_id=1, has_side_effects=True),
    )(parts)
    return total[None]


def solution(mesh):
    nx, ny = mesh.shape["blk"] // 4, mesh.shape["wide"] // NZ
    return jax.shard_map(
        functools.partial(shards, nx, ny),
        mesh=mesh,
        in_specs=(
            P("blk", "wide", None, None),
            P("blk", "wide", None, None),
            P("blk", "wide", None, None),
            P("blk", "wide", None),
            P("blk", "wide"),
            P("blk", "wide", None),
            P("blk", "wide"),
        ),
        out_specs=P("blk", "wide", None, None),
        check_vma=False,
    )
```

```python
import functools

import jax
import jax.numpy as jnp
from jax import lax
from jax.experimental import pallas as pl
from jax.experimental.pallas import tpu as pltpu
from jax.sharding import PartitionSpec as P

EPS2 = 0.04
MESH = pl.DeviceIdType.MESH
F32 = jnp.float32

NZ = 8
HALF = NZ // 2
AHEAD = NZ
SIBLING = AHEAD + HALF
SOURCES_Y = SIBLING + 2
MAX_PAIRS_ROWS = 6
SPLIT = 1


class Place:
    def __init__(self, nx, ny):
        self.nx, self.ny = nx, ny
        self.wide, self.blk = lax.axis_index("wide"), lax.axis_index("blk")
        self.y, self.z = self.wide // NZ, self.wide % NZ
        self.x, self.h, self.c = self.blk // 4, (self.blk // 2) % 2, self.blk % 2

    def at(self, y=None, z=None, x=None, h=None, c=None):
        pick = lambda given, mine: mine if given is None else given
        wide = pick(y, self.y) * NZ + pick(z, self.z)
        blk = pick(x, self.x) * 4 + pick(h, self.h) * 2 + pick(c, self.c)
        return {"wide": wide, "blk": blk}

    def beside(self, right):
        if right:
            crosses = (self.z == NZ - 1).astype(jnp.int32)
            z = (self.z + 1) % NZ
        else:
            crosses = (self.z == 0).astype(jnp.int32)
            z = (self.z + NZ - 1) % NZ
        return self.at(z=z, h=(self.h + crosses) % 2)

    def others_z(self):
        return [((self.z + d) % NZ, self.at(z=(self.z + d) % NZ)) for d in range(1, NZ)]

    def others_y(self):
        return [self.at(y=(self.y + d) % self.ny) for d in range(1, self.ny)]

    def others_x(self):
        return [((self.x + d) % self.nx, self.at(x=(self.x + d) % self.nx)) for d in range(1, self.nx)]

    def others_hc(self):
        return [self.at(h=(self.h + rel // 2) % 2, c=(self.c + rel % 2) % 2) for rel in (1, 2, 3)]


def greet(devices):
    barrier = pltpu.get_barrier_semaphore()
    for device in devices:
        pl.semaphore_signal(barrier, inc=1, device_id=device, device_id_type=MESH)


def await_greetings(count):
    pl.semaphore_wait(pltpu.get_barrier_semaphore(), count)


def near_mask(near, counts, width):
    blocks, listed = near.shape
    row = lax.broadcasted_iota(jnp.int32, (blocks, blocks), 0)
    own = row == lax.broadcasted_iota(jnp.int32, (blocks, blocks), 1)
    counts = jnp.sum(jnp.where(own, jnp.broadcast_to(counts, (blocks, blocks)), 0), axis=1, keepdims=True)
    lanes = lax.broadcasted_iota(jnp.int32, (blocks, width), 1)
    mask = jnp.zeros((blocks, width), F32)
    for n in range(listed):
        hit = jnp.where(near[:, n : n + 1] == lanes, 1.0, 0.0)
        mask = mask + jnp.where(counts > n, hit, 0.0)
    return mask


def pair_list(place, row_mask, col_mask):
    z, h, c, x, ny = place.z, place.h, place.c, place.x, place.ny
    sources_x = SOURCES_Y + ny
    rows, cols = row_mask.shape[0], col_mask.shape[0]
    own = rows + cols
    lane = lax.broadcasted_iota(jnp.int32, (128, 128), 0)
    k = lax.broadcasted_iota(jnp.int32, (128, 128), 1)
    rel = k // 4
    from_row = (k // 4) * (NZ * 4) + z * 4 + k % 4
    from_col = x * 16 + ((rel // 2 + h) % 2) * 8 + ((rel + c) % 2) * 4 + k % 4
    bf = jnp.bfloat16
    pick_row = jnp.where((lane == from_row) & (k < ny * 4), 1.0, 0.0).astype(bf)
    pick_col = jnp.where((lane == from_col) & (k < 16), 1.0, 0.0).astype(bf)
    dot = functools.partial(jnp.dot, preferred_element_type=F32)
    live = jnp.concatenate([dot(row_mask.astype(bf), pick_row), dot(col_mask.astype(bf), pick_col)], axis=0)
    before = dot(live.astype(bf), jnp.where(lane < k, 1.0, 0.0).astype(bf))
    totals = jnp.broadcast_to(jnp.sum(live, axis=1, keepdims=True), (own, 128))
    above = lax.broadcasted_iota(jnp.int32, (own, own), 0) > lax.broadcasted_iota(jnp.int32, (own, own), 1)
    offset = dot(jnp.where(above, 1.0, 0.0).astype(bf), totals.astype(bf))
    rank = jnp.where(live > 0.5, before + offset, -1.0)

    a = lax.broadcasted_iota(jnp.int32, (own, 128), 0)
    k = lax.broadcasted_iota(jnp.int32, (own, 128), 1)
    rel = k // 4
    unit = jnp.where(
        rel == 0, z, jnp.where(rel == 1, SIBLING, jnp.where(rel == 2, AHEAD + z % HALF, SIBLING + 1))
    )
    is_row = a < rows
    own_block = jnp.where(is_row, a, a - rows + sources_x * 4)
    far_block = jnp.where(is_row, SOURCES_Y * 4 + k, unit * 4 + k % 4)
    far_slot = jnp.where(is_row, k, ny * 4 + k)
    code = (own_block + 128 * far_block + 16384 * far_slot).astype(F32)

    fill = jnp.zeros((128 - own, 128), F32)
    rank_t = jnp.transpose(jnp.concatenate([rank, fill - 1.0], axis=0))[:16]
    code_t = jnp.transpose(jnp.concatenate([code, fill], axis=0))[:16]
    slots = lax.broadcasted_iota(jnp.int32, (16, 128), 1).astype(F32)
    packed = [jnp.zeros((16, 128), F32) for _ in range(MAX_PAIRS_ROWS)]
    for one in range(own):
        rank_one = jnp.broadcast_to(rank_t[:, one : one + 1], (16, 128))
        code_one = jnp.broadcast_to(code_t[:, one : one + 1], (16, 128))
        for r in range(MAX_PAIRS_ROWS):
            packed[r] = packed[r] + jnp.where(rank_one == slots + 128.0 * r, code_one, 0.0)
    listing = [jnp.sum(part, axis=0, keepdims=True) for part in packed]
    count = jnp.broadcast_to(jnp.sum(jnp.sum(live, axis=1, keepdims=True), axis=0, keepdims=True), (2, 128))
    return jnp.concatenate(listing + [count], axis=0).astype(jnp.int32)


def gather_kernel(
    nx,
    ny,
    source_ref,
    adjoint_ref,
    points_hbm,
    near_rows_hbm,
    counts_rows_hbm,
    near_cols_hbm,
    counts_cols_hbm,
    blocks_ref,
    meta_ref,
    far_axes_ref,
    list_ref,
    points_ref,
    near_rows_ref,
    counts_rows_ref,
    near_cols_ref,
    counts_cols_ref,
    own_meta,
    ring_send,
    ring_recv,
    core_send,
    core_recv,
    y_send,
    y_recv,
    x_send,
    x_recv,
    meta_send,
    meta_recv,
    local_sem,
    small_sem,
):
    smalls = [
        pltpu.make_async_copy(src, dst, small_sem.at[i])
        for i, (src, dst) in enumerate(
            (
                (points_hbm, points_ref),
                (near_rows_hbm, near_rows_ref),
                (counts_rows_hbm, counts_rows_ref),
                (near_cols_hbm, near_cols_ref),
                (counts_cols_hbm, counts_cols_ref),
            )
        )
    ]
    for copy in smalls:
        copy.start()
    place = Place(nx, ny)
    z, x, y = place.z, place.x, place.y
    per_device = source_ref.shape[0]
    sources_x = SOURCES_Y + ny
    right, left = place.beside(True), place.beside(False)
    sides = (right, left)
    others_z, others_y, others_x, others_hc = (
        place.others_z(),
        place.others_y(),
        place.others_x(),
        place.others_hc(),
    )
    sibling = others_hc[0]
    met = [device for _, device in others_z] + others_y + [device for _, device in others_x] + others_hc
    met = met + [right, left]
    greet(met)

    for copy in smalls:
        copy.wait()
    own_meta[...] = jnp.zeros_like(own_meta)
    row_mask = near_mask(near_rows_ref[...], counts_rows_ref[...], 128)
    col_mask = near_mask(near_cols_ref[...], counts_cols_ref[...], 128)
    points = [points_ref[c].astype(F32) for c in range(3)]
    for b in range(per_device):
        for c in range(3):
            own_meta[b, c : c + 1, :] = points[c][b : b + 1]
        own_meta[b, 4:5, :] = row_mask[b : b + 1]
        own_meta[b, 5:6, :] = col_mask[b : b + 1]

    await_greetings(len(met))

    def remote(src, dst, send, recv, device):
        return pltpu.make_async_remote_copy(
            src_ref=src, dst_ref=dst, send_sem=send, recv_sem=recv, device_id=device, device_id_type=MESH
        )

    def mirrored(side):
        return z if side == 0 else NZ - 1 - z

    def unit_of(side, m, t):
        near = m - 1 - t
        ahead = 3 - (t - m)
        if side == 0:
            return jnp.where(t < m, near, AHEAD + ahead)
        return jnp.where(t < m, NZ - 1 - near, AHEAD + 3 - ahead)

    def arrivals(m):
        return jnp.where(m < HALF, HALF, m)

    def forwards(m, t):
        last = m == NZ - 1
        return jnp.where(m < HALF, t < HALF - 1, jnp.where(last, t >= HALF - 1, True)) & (t < arrivals(m))

    def sent_unit(side, m, unit):
        crossed = AHEAD + unit if side == 0 else AHEAD + unit - HALF
        return jnp.where(m == NZ - 1, crossed, unit)

    def sent_number(m, t):
        return jnp.where(m == NZ - 1, t - (HALF - 1), t + 1)

    chunks = per_device * SPLIT
    depth = source_ref.shape[1] // SPLIT

    def part(ref, s):
        return ref.at[s // SPLIT, pl.ds(s % SPLIT * depth, depth)]

    def ring_copy(side, t, b):
        m = mirrored(side)
        unit = unit_of(side, m, t)
        return remote(
            part(blocks_ref.at[unit], b),
            part(blocks_ref.at[sent_unit(side, m, unit)], b),
            ring_send.at[side, t + 1, b],
            ring_recv.at[side, sent_number(m, t), b],
            sides[side],
        )

    def own_copy(side, b):
        return remote(
            part(adjoint_ref, b),
            part(blocks_ref.at[z], b),
            ring_send.at[side, 0, b],
            ring_recv.at[side, 0, b],
            sides[side],
        )

    def arrival(side, t, b):
        unit = unit_of(side, mirrored(side), t)
        slot = part(blocks_ref.at[unit], b)
        return remote(slot, slot, ring_send.at[side, t + 1, b], ring_recv.at[side, t, b], sides[side])

    def core_copy(b):
        return remote(
            part(blocks_ref.at[AHEAD + z % HALF], b),
            part(blocks_ref.at[SIBLING + 1], b),
            core_send.at[b],
            core_recv.at[b],
            sibling,
        )

    core_own = remote(
        adjoint_ref, blocks_ref.at[SIBLING], core_send.at[chunks], core_recv.at[chunks], sibling
    )

    for b in range(chunks):
        for side in (0, 1):

            @pl.when(mirrored(side) < NZ - 1)
            def _():
                own_copy(side, b).start()

    metas = []
    own_slots = [z, NZ + x, NZ + nx + y, NZ + nx + ny]
    for d, (_, device) in enumerate(others_z):
        metas.append((own_slots[0], d, device, (z + NZ - 1 - d) % NZ))
    for d, (_, device) in enumerate(others_x):
        metas.append((own_slots[1], NZ + d, device, NZ + (x + nx - 1 - d) % nx))
    for d, device in enumerate(others_y):
        metas.append((own_slots[2], NZ + nx + d, device, NZ + nx + (y + ny - 1 - d) % ny))
    for d, device in enumerate(others_hc):
        metas.append((NZ + nx + ny + 1 + d, NZ + nx + ny + d, device, NZ + nx + ny + 1 + d))
    meta_out = [
        remote(own_meta, meta_ref.at[slot], meta_send.at[s], meta_recv.at[s], device)
        for slot, s, device, _ in metas
    ]
    meta_in = [
        remote(own_meta, meta_ref.at[slot], meta_send.at[s], meta_recv.at[s], device)
        for _, s, device, slot in metas
    ]
    for copy in meta_out:
        copy.start()
    core_own.start()
    y_out, y_in, x_out, x_in = [], [], [], []
    for d, device in enumerate(others_y):
        sems = (y_send.at[d], y_recv.at[d], device)
        y_out.append(remote(source_ref, blocks_ref.at[SOURCES_Y + y], *sems))
        y_in.append(remote(source_ref, blocks_ref.at[SOURCES_Y + (y + ny - 1 - d) % ny], *sems))
    for d, (_, device) in enumerate(others_x):
        sems = (x_send.at[d], x_recv.at[d], device)
        x_out.append(remote(source_ref, blocks_ref.at[sources_x + x], *sems))
        x_in.append(remote(source_ref, blocks_ref.at[sources_x + (x + nx - 1 - d) % nx], *sems))
    for copy in y_out + x_out:
        copy.start()
    locals_ = [
        pltpu.make_async_copy(adjoint_ref, blocks_ref.at[z], local_sem.at[0]),
        pltpu.make_async_copy(source_ref, blocks_ref.at[SOURCES_Y + y], local_sem.at[1]),
        pltpu.make_async_copy(source_ref, blocks_ref.at[sources_x + x], local_sem.at[2]),
    ]
    for copy in locals_:
        copy.start()
    for slot in own_slots:
        meta_ref[slot] = own_meta[...]

    def due(m, hops):
        near = hops < m
        ahead = (m < HALF) & (hops >= HALF + m) & (hops < 2 * HALF)
        return near | ahead, jnp.where(near, hops, hops - HALF)

    def ring_step(s, carry):
        hops, b = s // chunks, s % chunks
        for side in (0, 1):
            m = mirrored(side)
            comes, t = due(m, hops)

            @pl.when(comes)
            def _():
                arrival(side, t, b).wait_recv()

                @pl.when(forwards(m, t))
                def _():
                    ring_copy(side, t, b).start()

                @pl.when((m < HALF) & (t == HALF - 1))
                def _():
                    core_copy(b).start()

        return carry

    lax.fori_loop(0, 2 * chunks, ring_step, 0)

    for copy in meta_in:
        copy.wait_recv()
    row_masks = jnp.concatenate([meta_ref[u, b, 4:5, :] for u in range(NZ) for b in range(per_device)], axis=0)
    col_masks = jnp.concatenate(
        [meta_ref[NZ + u, b, 5:6, :] for u in range(nx) for b in range(per_device)], axis=0
    )
    list_ref[...] = pair_list(place, row_masks, col_masks)

    fars = far_axes_ref.shape[0]
    first_far = NZ + nx
    steps = (NZ - 2) * chunks
    each = -(-fars // steps)
    axis = lax.broadcasted_iota(jnp.int32, (8, 3 * 128), 0)
    wanted = lax.broadcasted_iota(jnp.int32, (8, 3 * 128), 1) // 128
    spread = jnp.where(axis == wanted, 1.0, 0.0).astype(jnp.bfloat16)

    def spread_far(j):
        tile = meta_ref[first_far + j // per_device, j % per_device].astype(jnp.bfloat16)
        far_axes_ref[j] = lax.dot_general(
            tile, spread, (((0,), (0,)), ((), ())), preferred_element_type=F32
        )

    def ring_step_and_far(s, carry):
        ring_step(s, carry)
        for e in range(each):
            j = (s - 2 * chunks) * each + e

            @pl.when(j < fars)
            def _():
                spread_far(j)

        return carry

    lax.fori_loop(2 * chunks, NZ * chunks, ring_step_and_far, 0)

    for copy in y_in + x_in:
        copy.wait_recv()
    for b in range(chunks):
        core_copy(b).wait_recv()
    core_own.wait_recv()
    for copy in locals_:
        copy.wait()
    for copy in y_out + x_out + meta_out + [core_own]:
        copy.wait_send()
    for b in range(chunks):
        core_copy(b).wait_send()
        for side in (0, 1):

            @pl.when(mirrored(side) < NZ - 1)
            def _():
                own_copy(side, b).wait_send()

    def sent_step(s, carry):
        t, b = s // chunks, s % chunks
        for side in (0, 1):

            @pl.when(forwards(mirrored(side), t))
            def _():
                ring_copy(side, t, b).wait_send()

        return carry

    lax.fori_loop(0, (NZ - 1) * chunks, sent_step, 0)


UNROLL = 4


def pair_kernel(rows, own, shift, list_ref, blocks, meta_ref, far_axes, out_ref, acc):
    per_device = out_ref.shape[1] // 4
    acc[...] = jnp.zeros_like(acc)
    count = list_ref[MAX_PAIRS_ROWS, 0]

    def one_pair(k):
        code = list_ref[k // 128, k % 128]
        own_block, far_block, far_slot = code & 127, (code >> 7) & 127, code >> 14
        acc_slot = jnp.where(own_block < rows, own_block, own_block - shift)
        weights = lax.dot_general(
            blocks[far_block], blocks[own_block], (((1,), (1,)), ((), ())), preferred_element_type=F32
        )
        tile = meta_ref[acc_slot]
        own_axes = [jnp.broadcast_to(tile[c : c + 1], (8, 128)) for c in range(3)]
        sums = [jnp.zeros((8, 128), F32) for _ in range(3)]
        for r in range(16):
            at = slice(8 * r, 8 * r + 8)
            d = [far_axes[far_slot, at, 128 * c : 128 * c + 128] - own_axes[c] for c in range(3)]
            inverse = lax.rsqrt(d[0] * d[0] + d[1] * d[1] + d[2] * d[2] + EPS2)
            scaled = weights[at] * (inverse * inverse * inverse)
            sums = [sums[c] + d[c] * scaled for c in range(3)]
        return jnp.where(k < count, acc_slot, own), sums

    def step(i, carry):
        done = [one_pair(i * UNROLL + u) for u in range(UNROLL)]
        for slot, sums in done:
            for c in range(3):
                acc[slot, c] = acc[slot, c] + sums[c]
        return carry

    lax.fori_loop(0, (count + UNROLL - 1) // UNROLL, step, 0)
    out_ref[...] = jnp.zeros_like(out_ref)
    for a in range(own):
        for c in range(3):
            row = c * per_device + a % per_device
            out_ref[a // per_device, row : row + 1, :] = jnp.sum(acc[a, c], axis=0, keepdims=True)


def return_kernel(nx, ny, parts_ref, out_ref, landed, send_sem, recv_sem):
    place = Place(nx, ny)
    z, x = place.z, place.x
    others_z, others_x = place.others_z(), place.others_x()
    met = [device for _, device in others_z] + [device for _, device in others_x]
    greet(met)
    landed[z] = parts_ref[z]
    landed[NZ + x] = parts_ref[NZ + x]
    await_greetings(len(met))
    outgoing, incoming = [], []

    def both(s, theirs, mine, source, device):
        for slot, copies in ((mine, outgoing), (source, incoming)):
            copies.append(
                pltpu.make_async_remote_copy(
                    src_ref=parts_ref.at[theirs],
                    dst_ref=landed.at[slot],
                    send_sem=send_sem.at[s],
                    recv_sem=recv_sem.at[s],
                    device_id=device,
                    device_id_type=MESH,
                )
            )

    for d, (other, device) in enumerate(others_z):
        both(d, other, z, (z + NZ - 1 - d) % NZ, device)
    for d, (other, device) in enumerate(others_x):
        both(NZ + d, NZ + other, NZ + x, NZ + (x + nx - 1 - d) % nx, device)
    for copy in outgoing:
        copy.start()
    for copy in incoming:
        copy.wait_recv()
    total = landed[0]
    for u in range(1, NZ + nx):
        total = total + landed[u]
    per_device = out_ref.shape[1]
    for c in range(3):
        out_ref[c] = total[c * per_device : (c + 1) * per_device]
    for copy in outgoing:
        copy.wait_send()


def shards(
    nx,
    ny,
    source_strength,
    adjoint_strength,
    node_points,
    near_rows,
    counts_rows,
    near_cols,
    counts_cols,
):
    _, per_device, size_block, conditions = source_strength.shape
    units = SOURCES_Y + ny + nx
    metas = NZ + nx + ny + 4
    dma = pltpu.SemaphoreType.DMA
    any_space = pl.BlockSpec(memory_space=pl.ANY)
    hbm = pl.BlockSpec(memory_space=pltpu.HBM)
    fars = (ny + 4) * per_device
    small = pltpu.CompilerParams(vmem_limit_bytes=8 * 1024 * 1024)
    vmem = pl.BlockSpec(memory_space=pltpu.VMEM)
    blocks, meta, far_axes, listing = pl.pallas_call(
        functools.partial(gather_kernel, nx, ny),
        name="gather",
        out_shape=(
            jax.ShapeDtypeStruct((units, per_device, size_block, conditions), jnp.bfloat16),
            jax.ShapeDtypeStruct((metas, per_device, 8, 128), F32),
            jax.ShapeDtypeStruct((fars, size_block, 3 * 128), F32),
            jax.ShapeDtypeStruct((8, 128), jnp.int32),
        ),
        in_specs=[hbm] * 7,
        out_specs=(any_space, vmem, vmem, vmem),
        scratch_shapes=[
            pltpu.VMEM((3, per_device, size_block), jnp.bfloat16),
            pltpu.VMEM((per_device, near_rows.shape[2]), jnp.int32),
            pltpu.VMEM((1, per_device), jnp.int32),
            pltpu.VMEM((per_device, near_cols.shape[2]), jnp.int32),
            pltpu.VMEM((1, per_device), jnp.int32),
            pltpu.VMEM((per_device, 8, 128), F32),
            dma((2, NZ, per_device * SPLIT)),
            dma((2, NZ, per_device * SPLIT)),
            dma((per_device * SPLIT + 1,)),
            dma((per_device * SPLIT + 1,)),
            dma((max(ny - 1, 1),)),
            dma((max(ny - 1, 1),)),
            dma((max(nx - 1, 1),)),
            dma((max(nx - 1, 1),)),
            dma((metas,)),
            dma((metas,)),
            dma((3,)),
            dma((5,)),
        ],
        compiler_params=pltpu.CompilerParams(
            collective_id=0, has_side_effects=True, vmem_limit_bytes=16 * 1024 * 1024
        ),
    )(
        *(
            pltpu.with_memory_space_constraint(operand, pltpu.HBM)
            for operand in (
                source_strength[0],
                adjoint_strength[0],
                jnp.transpose(node_points[0], (1, 0, 2)),
                near_rows[0],
                counts_rows,
                near_cols[0],
                counts_cols,
            )
        )
    )
    rows = NZ * per_device
    own = rows + nx * per_device
    shift = (SOURCES_Y + ny) * per_device - rows
    parts = pl.pallas_call(
        functools.partial(pair_kernel, rows, own, shift),
        name="pairs",
        out_shape=jax.ShapeDtypeStruct((NZ + nx, 4 * per_device, 128), F32),
        in_specs=[pl.BlockSpec(memory_space=pltpu.SMEM), vmem, vmem, vmem],
        out_specs=vmem,
        scratch_shapes=[pltpu.VMEM((own + 1, 3, 8, 128), F32)],
        compiler_params=small,
    )(
        listing,
        blocks.reshape(units * per_device, size_block, conditions),
        meta.reshape(metas * per_device, 8, 128),
        far_axes,
    )
    total = pl.pallas_call(
        functools.partial(return_kernel, nx, ny),
        name="sums",
        out_shape=jax.ShapeDtypeStruct((3, per_device, 128), F32),
        in_specs=[vmem],
        out_specs=vmem,
        scratch_shapes=[
            pltpu.VMEM((NZ + nx, 4 * per_device, 128), F32),
            dma((NZ + nx,)),
            dma((NZ + nx,)),
        ],
        compiler_params=pltpu.CompilerParams(
            collective_id=1, has_side_effects=True, vmem_limit_bytes=8 * 1024 * 1024
        ),
    )(parts)
    return jnp.transpose(total, (1, 0, 2))[None]


def solution(mesh):
    nx, ny = mesh.shape["blk"] // 4, mesh.shape["wide"] // NZ
    return jax.shard_map(
        functools.partial(shards, nx, ny),
        mesh=mesh,
        in_specs=(
            P("blk", "wide", None, None),
            P("blk", "wide", None, None),
            P("blk", "wide", None, None),
            P("blk", "wide", None),
            P("blk", "wide"),
            P("blk", "wide", None),
            P("blk", "wide"),
        ),
        out_specs=P("blk", "wide", None, None),
        check_vma=False,
    )
```

```python
import functools

import jax
import jax.numpy as jnp
from jax import lax
from jax.experimental import pallas as pl
from jax.experimental.pallas import tpu as pltpu
from jax.sharding import PartitionSpec as P

EPS2 = 0.04
MESH = pl.DeviceIdType.MESH
F32 = jnp.float32

NZ = 8
HALF = NZ // 2
AHEAD = NZ
SIBLING = AHEAD + HALF
SOURCES_Y = SIBLING + 2
MAX_PAIRS_ROWS = 6
SPLIT = 1
MET_AT = 8
LISTED_AT = 28, 28


class Place:
    def __init__(self, nx, ny):
        self.nx, self.ny = nx, ny
        self.wide, self.blk = lax.axis_index("wide"), lax.axis_index("blk")
        self.y, self.z = self.wide // NZ, self.wide % NZ
        self.x, self.h, self.c = self.blk // 4, (self.blk // 2) % 2, self.blk % 2

    def at(self, y=None, z=None, x=None, h=None, c=None):
        pick = lambda given, mine: mine if given is None else given
        wide = pick(y, self.y) * NZ + pick(z, self.z)
        blk = pick(x, self.x) * 4 + pick(h, self.h) * 2 + pick(c, self.c)
        return {"wide": wide, "blk": blk}

    def beside(self, right):
        if right:
            crosses = (self.z == NZ - 1).astype(jnp.int32)
            z = (self.z + 1) % NZ
        else:
            crosses = (self.z == 0).astype(jnp.int32)
            z = (self.z + NZ - 1) % NZ
        return self.at(z=z, h=(self.h + crosses) % 2)

    def others_z(self):
        return [((self.z + d) % NZ, self.at(z=(self.z + d) % NZ)) for d in range(1, NZ)]

    def others_y(self):
        return [self.at(y=(self.y + d) % self.ny) for d in range(1, self.ny)]

    def others_x(self):
        return [((self.x + d) % self.nx, self.at(x=(self.x + d) % self.nx)) for d in range(1, self.nx)]

    def others_hc(self):
        return [self.at(h=(self.h + rel // 2) % 2, c=(self.c + rel % 2) % 2) for rel in (1, 2, 3)]


def greet(devices):
    barrier = pltpu.get_barrier_semaphore()
    for device in devices:
        pl.semaphore_signal(barrier, inc=1, device_id=device, device_id_type=MESH)


def await_greetings(count):
    pl.semaphore_wait(pltpu.get_barrier_semaphore(), count)


def near_mask(near, counts, width):
    blocks, listed = near.shape
    row = lax.broadcasted_iota(jnp.int32, (blocks, blocks), 0)
    own = row == lax.broadcasted_iota(jnp.int32, (blocks, blocks), 1)
    counts = jnp.sum(jnp.where(own, jnp.broadcast_to(counts, (blocks, blocks)), 0), axis=1, keepdims=True)
    lanes = lax.broadcasted_iota(jnp.int32, (blocks, width), 1)
    mask = jnp.zeros((blocks, width), F32)
    for n in range(listed):
        hit = jnp.where(near[:, n : n + 1] == lanes, 1.0, 0.0)
        mask = mask + jnp.where(counts > n, hit, 0.0)
    return mask


def pair_list(place, row_mask, col_mask):
    z, h, c, x, ny = place.z, place.h, place.c, place.x, place.ny
    sources_x = SOURCES_Y + ny
    rows, cols = row_mask.shape[0], col_mask.shape[0]
    own = rows + cols
    lane = lax.broadcasted_iota(jnp.int32, (128, 128), 0)
    k = lax.broadcasted_iota(jnp.int32, (128, 128), 1)
    rel = k // 4
    from_row = (k // 4) * (NZ * 4) + z * 4 + k % 4
    from_col = x * 16 + ((rel // 2 + h) % 2) * 8 + ((rel + c) % 2) * 4 + k % 4
    bf = jnp.bfloat16
    pick_row = jnp.where((lane == from_row) & (k < ny * 4), 1.0, 0.0).astype(bf)
    pick_col = jnp.where((lane == from_col) & (k < 16), 1.0, 0.0).astype(bf)
    dot = functools.partial(jnp.dot, preferred_element_type=F32)
    live = jnp.concatenate([dot(row_mask.astype(bf), pick_row), dot(col_mask.astype(bf), pick_col)], axis=0)
    before = dot(live.astype(bf), jnp.where(lane < k, 1.0, 0.0).astype(bf))
    totals = jnp.broadcast_to(jnp.sum(live, axis=1, keepdims=True), (own, 128))
    above = lax.broadcasted_iota(jnp.int32, (own, own), 0) > lax.broadcasted_iota(jnp.int32, (own, own), 1)
    offset = dot(jnp.where(above, 1.0, 0.0).astype(bf), totals.astype(bf))
    rank = jnp.where(live > 0.5, before + offset, -1.0)

    a = lax.broadcasted_iota(jnp.int32, (own, 128), 0)
    k = lax.broadcasted_iota(jnp.int32, (own, 128), 1)
    rel = k // 4
    unit = jnp.where(
        rel == 0, z, jnp.where(rel == 1, SIBLING, jnp.where(rel == 2, AHEAD + z % HALF, SIBLING + 1))
    )
    is_row = a < rows
    own_block = jnp.where(is_row, a, a - rows + sources_x * 4)
    far_block = jnp.where(is_row, SOURCES_Y * 4 + k, unit * 4 + k % 4)
    far_slot = jnp.where(is_row, k, ny * 4 + k)
    code = (own_block + 128 * far_block + 16384 * far_slot).astype(F32)

    fill = jnp.zeros((128 - own, 128), F32)
    rank_t = jnp.transpose(jnp.concatenate([rank, fill - 1.0], axis=0))[:16]
    code_t = jnp.transpose(jnp.concatenate([code, fill], axis=0))[:16]
    slots = lax.broadcasted_iota(jnp.int32, (16, 128), 1).astype(F32)
    packed = [jnp.zeros((16, 128), F32) for _ in range(MAX_PAIRS_ROWS)]
    for one in range(own):
        rank_one = jnp.broadcast_to(rank_t[:, one : one + 1], (16, 128))
        code_one = jnp.broadcast_to(code_t[:, one : one + 1], (16, 128))
        for r in range(MAX_PAIRS_ROWS):
            packed[r] = packed[r] + jnp.where(rank_one == slots + 128.0 * r, code_one, 0.0)
    listing = [jnp.sum(part, axis=0, keepdims=True) for part in packed]
    count = jnp.broadcast_to(jnp.sum(jnp.sum(live, axis=1, keepdims=True), axis=0, keepdims=True), (2, 128))
    return jnp.concatenate(listing + [count], axis=0).astype(jnp.int32)


def gather_kernel(
    nx,
    ny,
    source_ref,
    adjoint_ref,
    points_hbm,
    near_rows_hbm,
    counts_rows_hbm,
    near_cols_hbm,
    counts_cols_hbm,
    blocks_ref,
    own_axes_ref,
    far_axes_ref,
    list_ref,
    points_ref,
    near_rows_ref,
    counts_rows_ref,
    near_cols_ref,
    counts_cols_ref,
    own_meta,
    meta_ref,
    through_send,
    through_recv,
    extra_send,
    extra_recv,
    core_send,
    core_recv,
    y_send,
    y_recv,
    x_send,
    x_recv,
    meta_send,
    meta_recv,
    local_sem,
    small_sem,
):
    smalls = [
        pltpu.make_async_copy(src, dst, small_sem.at[i])
        for i, (src, dst) in enumerate(
            (
                (points_hbm, points_ref),
                (near_rows_hbm, near_rows_ref),
                (counts_rows_hbm, counts_rows_ref),
                (near_cols_hbm, near_cols_ref),
                (counts_cols_hbm, counts_cols_ref),
            )
        )
    ]
    for copy in smalls:
        copy.start()
    place = Place(nx, ny)
    z, x, y = place.z, place.x, place.y
    per_device = source_ref.shape[0]
    sources_x = SOURCES_Y + ny
    right, left = place.beside(True), place.beside(False)
    sides = (right, left)
    others_z, others_y, others_x, others_hc = (
        place.others_z(),
        place.others_y(),
        place.others_x(),
        place.others_hc(),
    )
    sibling = others_hc[0]
    met = [device for _, device in others_z] + others_y + [device for _, device in others_x] + others_hc
    met = met + [right, left]
    greet(met)

    for copy in smalls:
        copy.wait()
    points = points_ref[...].astype(F32).reshape(3 * per_device, 128)
    row_mask = near_mask(near_rows_ref[...], counts_rows_ref[...], 128)
    col_mask = near_mask(near_cols_ref[...], counts_cols_ref[...], 128)
    for which, mask in enumerate((row_mask, col_mask)):
        own_meta[which] = jnp.concatenate([points, mask], axis=0).astype(jnp.bfloat16)

    await_greetings(len(met))

    def remote(src, dst, send, recv, device):
        return pltpu.make_async_remote_copy(
            src_ref=src, dst_ref=dst, send_sem=send, recv_sem=recv, device_id=device, device_id_type=MESH
        )

    chunks = per_device * SPLIT
    depth = source_ref.shape[1] // SPLIT
    hop = 3 * chunks // 4

    def part(ref, s):
        return ref.at[s // SPLIT, pl.ds(s % SPLIT * depth, depth)]

    def mirrored(side):
        return z if side == 0 else NZ - 1 - z

    def slot_of(side, unit):
        return unit if side == 0 else NZ - 1 - unit

    def through_unit(side, m, t):
        near = jnp.where(m < HALF, m - 1 - t, HALF - 1 - t)
        ahead = HALF - 1 - (t - m)
        is_near = (m >= HALF) | (t < m)
        return jnp.where(is_near, slot_of(side, near), AHEAD + (ahead if side == 0 else HALF - 1 - ahead))

    def passes_on(m, t):
        return (m >= HALF) | (t < HALF - 1)

    def through_copy(side, t, b):
        m = mirrored(side)
        unit = through_unit(side, m, t)
        crossed = AHEAD + unit if side == 0 else AHEAD + unit - HALF
        return remote(
            part(blocks_ref.at[unit], b),
            part(blocks_ref.at[jnp.where(m == NZ - 1, crossed, unit)], b),
            through_send.at[side, t + 1, b],
            through_recv.at[side, jnp.where(m < HALF, t + 1, t), b],
            sides[side],
        )

    def through_arrival(side, t, b):
        slot = part(blocks_ref.at[through_unit(side, mirrored(side), t)], b)
        return remote(slot, slot, through_send.at[side, t + 1, b], through_recv.at[side, t, b], sides[side])

    def extra_copy(side, e, b):
        slot = part(blocks_ref.at[slot_of(side, mirrored(side) - 1 - e)], b)
        return remote(slot, slot, extra_send.at[side, e + 1, b], extra_recv.at[side, e + 1, b], sides[side])

    def extra_arrival(side, e, b):
        slot = part(blocks_ref.at[slot_of(side, mirrored(side) - 1 - e)], b)
        return remote(slot, slot, extra_send.at[side, e + 1, b], extra_recv.at[side, e, b], sides[side])

    def own_copy(side, b):
        send, recv = through_send.at[side, 0, b], through_recv.at[side, 0, b]
        return remote(part(adjoint_ref, b), part(blocks_ref.at[z], b), send, recv, sides[side])

    def own_extra_copy(side, b):
        send, recv = extra_send.at[side, 0, b], extra_recv.at[side, 0, b]
        return remote(part(adjoint_ref, b), part(blocks_ref.at[z], b), send, recv, sides[side])

    def sends_extra(m):
        return (m >= HALF) & (m < NZ - 1)

    def core_copy(b):
        return remote(
            part(blocks_ref.at[AHEAD + z % HALF], b),
            part(blocks_ref.at[SIBLING + 1], b),
            core_send.at[b],
            core_recv.at[b],
            sibling,
        )

    core_own = remote(
        adjoint_ref, blocks_ref.at[SIBLING], core_send.at[chunks], core_recv.at[chunks], sibling
    )

    for b in range(chunks):
        for side in (0, 1):
            m = mirrored(side)

            @pl.when(m < HALF)
            def _():
                own_copy(side, b).start()

            @pl.when(sends_extra(m) & ((m > HALF) | (b < hop)))
            def _():
                own_extra_copy(side, b).start()

    metas = []
    own_slots = [z, NZ + x, NZ + nx + y, NZ + nx + ny]
    for d, (_, device) in enumerate(others_z):
        metas.append((0, own_slots[0], d, device, (z + NZ - 1 - d) % NZ))
    for d, (_, device) in enumerate(others_x):
        metas.append((1, own_slots[1], NZ + d, device, NZ + (x + nx - 1 - d) % nx))
    for d, device in enumerate(others_y):
        metas.append((1, own_slots[2], NZ + nx + d, device, NZ + nx + (y + ny - 1 - d) % ny))
    for d, device in enumerate(others_hc):
        metas.append((1, NZ + nx + ny + 1 + d, NZ + nx + ny + d, device, NZ + nx + ny + 1 + d))
    meta_out = [
        remote(own_meta.at[which], meta_ref.at[slot], meta_send.at[s], meta_recv.at[s], device)
        for which, slot, s, device, _ in metas
    ]
    meta_in = [
        remote(own_meta.at[which], meta_ref.at[slot], meta_send.at[s], meta_recv.at[s], device)
        for which, _, s, device, slot in metas
    ]
    for copy in meta_out:
        copy.start()
    core_own.start()
    y_out, y_in, x_out, x_in = [], [], [], []
    for d, device in enumerate(others_y):
        sems = (y_send.at[d], y_recv.at[d], device)
        y_out.append(remote(source_ref, blocks_ref.at[SOURCES_Y + y], *sems))
        y_in.append(remote(source_ref, blocks_ref.at[SOURCES_Y + (y + ny - 1 - d) % ny], *sems))
    for d, (_, device) in enumerate(others_x):
        sems = (x_send.at[d], x_recv.at[d], device)
        x_out.append(remote(source_ref, blocks_ref.at[sources_x + x], *sems))
        x_in.append(remote(source_ref, blocks_ref.at[sources_x + (x + nx - 1 - d) % nx], *sems))
    for copy in y_out + x_out:
        copy.start()
    locals_ = [
        pltpu.make_async_copy(adjoint_ref, blocks_ref.at[z], local_sem.at[0]),
        pltpu.make_async_copy(source_ref, blocks_ref.at[SOURCES_Y + y], local_sem.at[1]),
        pltpu.make_async_copy(source_ref, blocks_ref.at[sources_x + x], local_sem.at[2]),
    ]
    for copy in locals_:
        copy.start()
    for which, slot in zip((0, 1, 1, 1), own_slots):
        meta_ref[slot] = own_meta[which]

    def ring_step(s, carry):
        for side in (0, 1):
            m = mirrored(side)
            far = s - hop * (m - HALF + 1)
            near = s - hop
            ahead = s - hop * (HALF + 1) + (chunks - hop) * m
            is_near = near < chunks * m
            q = jnp.where(m >= HALF, far, jnp.where(is_near, near, ahead))
            comes = (q >= 0) & (q < HALF * chunks) & ((m >= HALF) | is_near | (ahead >= chunks * m))
            t, b = jnp.maximum(q, 0) // chunks, jnp.maximum(q, 0) % chunks

            @pl.when(comes)
            def _():
                through_arrival(side, t, b).wait_recv()

                @pl.when(passes_on(m, t))
                def _():
                    through_copy(side, t, b).start()

                @pl.when((m < HALF) & (t == HALF - 1))
                def _():
                    core_copy(b).start()

            late = far - HALF * chunks
            is_late = (m > HALF) & (m < NZ - 1) & (late >= 0) & (late < chunks)
            is_early = (m == NZ - 2) & (near >= 0) & (near < chunks)

            @pl.when(is_late | is_early)
            def _():
                e = jnp.where(is_late & (m == NZ - 2), 1, 0)
                b = jnp.where(is_late, late, near)
                extra_arrival(side, e, b).wait_recv()
                extra_copy(side, e, b).start()

            @pl.when((m == HALF) & (late == 0))
            def _():
                for b in range(hop, chunks):
                    own_extra_copy(side, b).start()

        return carry

    slots = (HALF + 1) * hop + HALF * chunks
    fars = far_axes_ref.shape[0]
    first_far = NZ + nx
    each = -(-fars // (slots - MET_AT - 1))
    at_end = (z == 0) | (z == NZ - 1)
    listed_at = jnp.where(at_end, LISTED_AT[0], LISTED_AT[1])
    axis = lax.broadcasted_iota(jnp.int32, (4 * per_device, 3 * 128), 0)
    wanted = lax.broadcasted_iota(jnp.int32, (4 * per_device, 3 * 128), 1) // 128 * per_device

    def spread_far(j):
        spread = jnp.where(axis == wanted + j % per_device, 1.0, 0.0).astype(jnp.bfloat16)
        far_axes_ref[j] = lax.dot_general(
            meta_ref[first_far + j // per_device], spread, (((0,), (0,)), ((), ())), preferred_element_type=F32
        )

    def list_pairs():
        masks = [meta_ref[u].astype(F32)[3 * per_device :] for u in range(NZ + nx)]
        row_masks = jnp.concatenate(masks[:NZ], axis=0)
        col_masks = jnp.concatenate(masks[NZ:], axis=0)
        list_ref[...] = pair_list(place, row_masks, col_masks)
        for u in range(NZ + nx):
            tile = meta_ref[u].astype(F32)
            for b in range(per_device):
                for c in range(3):
                    row = c * per_device + b
                    own_axes_ref[u * per_device + b, c : c + 1, :] = tile[row : row + 1]

    def ring_and_more(s, carry):
        ring_step(s, carry)

        @pl.when(s == MET_AT)
        def _():
            for copy in meta_in:
                copy.wait_recv()

        @pl.when(s == listed_at)
        def _():
            list_pairs()

        for e in range(each):
            j = (s - MET_AT - 1) * each + e

            @pl.when((j >= 0) & (j < fars))
            def _():
                spread_far(j)

        return carry

    lax.fori_loop(hop, slots, ring_and_more, 0)

    for side in (0, 1):

        @pl.when(mirrored(side) == NZ - 1)
        def _():
            def kept(s, carry):
                extra_arrival(side, s // chunks, s % chunks).wait_recv()
                return carry

            lax.fori_loop(0, (HALF - 1) * chunks, kept, 0)


    for copy in y_in + x_in:
        copy.wait_recv()
    for b in range(chunks):
        core_copy(b).wait_recv()
    core_own.wait_recv()
    for copy in locals_:
        copy.wait()
    for copy in y_out + x_out + meta_out + [core_own]:
        copy.wait_send()
    def sent(b, carry):
        core_copy(b).wait_send()
        for side in (0, 1):
            m = mirrored(side)

            @pl.when(m < HALF)
            def _():
                own_copy(side, b).wait_send()

            @pl.when(sends_extra(m))
            def _():
                own_extra_copy(side, b).wait_send()

            for t in range(HALF):

                @pl.when(passes_on(m, t))
                def _():
                    through_copy(side, t, b).wait_send()

            for e in range(2):

                @pl.when((m > HALF + e) & (m < NZ - 1))
                def _():
                    extra_copy(side, e, b).wait_send()

        return carry

    lax.fori_loop(0, chunks, sent, 0)


UNROLL = 8


def pair_kernel(rows, own, shift, list_ref, blocks, own_axes_ref, far_axes, out_ref, acc):
    per_device = out_ref.shape[1] // 4
    acc[...] = jnp.zeros_like(acc)
    count = list_ref[MAX_PAIRS_ROWS, 0]

    def one_pair(k):
        code = list_ref[k // 128, k % 128]
        own_block, far_block, far_slot = code & 127, (code >> 7) & 127, code >> 14
        acc_slot = jnp.where(own_block < rows, own_block, own_block - shift)
        weights = lax.dot_general(
            blocks[far_block], blocks[own_block], (((1,), (1,)), ((), ())), preferred_element_type=F32
        )
        tile = own_axes_ref[acc_slot]
        own_axes = [jnp.broadcast_to(tile[c : c + 1], (8, 128)) for c in range(3)]
        sums = [jnp.zeros((8, 128), F32) for _ in range(3)]
        for r in range(16):
            at = slice(8 * r, 8 * r + 8)
            d = [far_axes[far_slot, at, 128 * c : 128 * c + 128] - own_axes[c] for c in range(3)]
            inverse = lax.rsqrt(d[0] * d[0] + d[1] * d[1] + d[2] * d[2] + EPS2)
            scaled = weights[at] * (inverse * inverse * inverse)
            sums = [sums[c] + d[c] * scaled for c in range(3)]
        return jnp.where(k < count, acc_slot, own), sums

    def step(i, carry):
        done = [one_pair(i * UNROLL + u) for u in range(UNROLL)]
        for slot, sums in done:
            for c in range(3):
                acc[slot, c] = acc[slot, c] + sums[c]
        return carry

    lax.fori_loop(0, (count + UNROLL - 1) // UNROLL, step, 0)
    out_ref[...] = jnp.zeros_like(out_ref)
    for a in range(own):
        for c in range(3):
            row = c * per_device + a % per_device
            out_ref[a // per_device, row : row + 1, :] = jnp.sum(acc[a, c], axis=0, keepdims=True)


def return_kernel(nx, ny, parts_ref, out_ref, landed, send_sem, recv_sem):
    place = Place(nx, ny)
    z, x = place.z, place.x
    others_z, others_x = place.others_z(), place.others_x()
    met = [device for _, device in others_z] + [device for _, device in others_x]
    greet(met)
    landed[z] = parts_ref[z]
    landed[NZ + x] = parts_ref[NZ + x]
    await_greetings(len(met))
    outgoing, incoming = [], []

    def both(s, theirs, mine, source, device):
        for slot, copies in ((mine, outgoing), (source, incoming)):
            copies.append(
                pltpu.make_async_remote_copy(
                    src_ref=parts_ref.at[theirs],
                    dst_ref=landed.at[slot],
                    send_sem=send_sem.at[s],
                    recv_sem=recv_sem.at[s],
                    device_id=device,
                    device_id_type=MESH,
                )
            )

    for d, (other, device) in enumerate(others_z):
        both(d, other, z, (z + NZ - 1 - d) % NZ, device)
    for d, (other, device) in enumerate(others_x):
        both(NZ + d, NZ + other, NZ + x, NZ + (x + nx - 1 - d) % nx, device)
    for copy in outgoing:
        copy.start()
    for copy in incoming:
        copy.wait_recv()
    total = landed[0]
    for u in range(1, NZ + nx):
        total = total + landed[u]
    per_device = out_ref.shape[1]
    for c in range(3):
        out_ref[c] = total[c * per_device : (c + 1) * per_device]
    for copy in outgoing:
        copy.wait_send()


def shards(
    nx,
    ny,
    source_strength,
    adjoint_strength,
    node_points,
    near_rows,
    counts_rows,
    near_cols,
    counts_cols,
):
    _, per_device, size_block, conditions = source_strength.shape
    units = SOURCES_Y + ny + nx
    metas = NZ + nx + ny + 4
    dma = pltpu.SemaphoreType.DMA
    any_space = pl.BlockSpec(memory_space=pl.ANY)
    hbm = pl.BlockSpec(memory_space=pltpu.HBM)
    fars = (ny + 4) * per_device
    small = pltpu.CompilerParams(vmem_limit_bytes=8 * 1024 * 1024)
    vmem = pl.BlockSpec(memory_space=pltpu.VMEM)
    blocks, own_axes, far_axes, listing = pl.pallas_call(
        functools.partial(gather_kernel, nx, ny),
        name="gather",
        out_shape=(
            jax.ShapeDtypeStruct((units, per_device, size_block, conditions), jnp.bfloat16),
            jax.ShapeDtypeStruct(((NZ + nx) * per_device, 8, 128), F32),
            jax.ShapeDtypeStruct((fars, size_block, 3 * 128), F32),
            jax.ShapeDtypeStruct((8, 128), jnp.int32),
        ),
        in_specs=[hbm] * 7,
        out_specs=(any_space, vmem, vmem, vmem),
        scratch_shapes=[
            pltpu.VMEM((3, per_device, size_block), jnp.bfloat16),
            pltpu.VMEM((per_device, near_rows.shape[2]), jnp.int32),
            pltpu.VMEM((1, per_device), jnp.int32),
            pltpu.VMEM((per_device, near_cols.shape[2]), jnp.int32),
            pltpu.VMEM((1, per_device), jnp.int32),
            pltpu.VMEM((2, 4 * per_device, 128), jnp.bfloat16),
            pltpu.VMEM((metas, 4 * per_device, 128), jnp.bfloat16),
            dma((2, HALF + 1, per_device * SPLIT)),
            dma((2, HALF, per_device * SPLIT)),
            dma((2, HALF, per_device * SPLIT)),
            dma((2, HALF, per_device * SPLIT)),
            dma((per_device * SPLIT + 1,)),
            dma((per_device * SPLIT + 1,)),
            dma((max(ny - 1, 1),)),
            dma((max(ny - 1, 1),)),
            dma((max(nx - 1, 1),)),
            dma((max(nx - 1, 1),)),
            dma((metas,)),
            dma((metas,)),
            dma((3,)),
            dma((5,)),
        ],
        compiler_params=pltpu.CompilerParams(
            collective_id=0, has_side_effects=True, vmem_limit_bytes=16 * 1024 * 1024
        ),
    )(
        *(
            pltpu.with_memory_space_constraint(operand, pltpu.HBM)
            for operand in (
                source_strength[0],
                adjoint_strength[0],
                jnp.transpose(node_points[0], (1, 0, 2)),
                near_rows[0],
                counts_rows,
                near_cols[0],
                counts_cols,
            )
        )
    )
    rows = NZ * per_device
    own = rows + nx * per_device
    shift = (SOURCES_Y + ny) * per_device - rows
    parts = pl.pallas_call(
        functools.partial(pair_kernel, rows, own, shift),
        name="pairs",
        out_shape=jax.ShapeDtypeStruct((NZ + nx, 4 * per_device, 128), F32),
        in_specs=[pl.BlockSpec(memory_space=pltpu.SMEM), vmem, vmem, vmem],
        out_specs=vmem,
        scratch_shapes=[pltpu.VMEM((own + 1, 3, 8, 128), F32)],
        compiler_params=small,
    )(
        listing,
        blocks.reshape(units * per_device, size_block, conditions),
        own_axes,
        far_axes,
    )
    total = pl.pallas_call(
        functools.partial(return_kernel, nx, ny),
        name="sums",
        out_shape=jax.ShapeDtypeStruct((3, per_device, 128), F32),
        in_specs=[vmem],
        out_specs=vmem,
        scratch_shapes=[
            pltpu.VMEM((NZ + nx, 4 * per_device, 128), F32),
            dma((NZ + nx,)),
            dma((NZ + nx,)),
        ],
        compiler_params=pltpu.CompilerParams(
            collective_id=1, has_side_effects=True, vmem_limit_bytes=8 * 1024 * 1024
        ),
    )(parts)
    return jnp.transpose(total, (1, 0, 2))[None]


def solution(mesh):
    nx, ny = mesh.shape["blk"] // 4, mesh.shape["wide"] // NZ
    return jax.shard_map(
        functools.partial(shards, nx, ny),
        mesh=mesh,
        in_specs=(
            P("blk", "wide", None, None),
            P("blk", "wide", None, None),
            P("blk", "wide", None, None),
            P("blk", "wide", None),
            P("blk", "wide"),
            P("blk", "wide", None),
            P("blk", "wide"),
        ),
        out_specs=P("blk", "wide", None, None),
        check_vma=False,
    )
```

```python
import functools

import jax
import jax.numpy as jnp
from jax import lax
from jax.experimental import pallas as pl
from jax.experimental.pallas import tpu as pltpu
from jax.sharding import PartitionSpec as P

EPS2 = 0.04
MESH = pl.DeviceIdType.MESH
F32 = jnp.float32

NZ = 8
HALF = NZ // 2
AHEAD = NZ
SIBLING = AHEAD + HALF
SOURCES_Y = SIBLING + 2
COLS_AT = 4
MAX_PAIRS_ROWS = 6
SPLIT = 1
MET_AT = 8
LISTED_AT = 28, 28


class Place:
    def __init__(self, nx, ny):
        self.nx, self.ny = nx, ny
        self.wide, self.blk = lax.axis_index("wide"), lax.axis_index("blk")
        self.y, self.z = self.wide // NZ, self.wide % NZ
        self.x, self.h, self.c = self.blk // 4, (self.blk // 2) % 2, self.blk % 2

    def at(self, y=None, z=None, x=None, h=None, c=None):
        pick = lambda given, mine: mine if given is None else given
        wide = pick(y, self.y) * NZ + pick(z, self.z)
        blk = pick(x, self.x) * 4 + pick(h, self.h) * 2 + pick(c, self.c)
        return {"wide": wide, "blk": blk}

    def beside(self, right):
        if right:
            crosses = (self.z == NZ - 1).astype(jnp.int32)
            z = (self.z + 1) % NZ
        else:
            crosses = (self.z == 0).astype(jnp.int32)
            z = (self.z + NZ - 1) % NZ
        return self.at(z=z, h=(self.h + crosses) % 2)

    def others_z(self):
        return [((self.z + d) % NZ, self.at(z=(self.z + d) % NZ)) for d in range(1, NZ)]

    def others_y(self):
        return [self.at(y=(self.y + d) % self.ny) for d in range(1, self.ny)]

    def others_x(self):
        return [((self.x + d) % self.nx, self.at(x=(self.x + d) % self.nx)) for d in range(1, self.nx)]

    def others_hc(self):
        return [self.at(h=(self.h + rel // 2) % 2, c=(self.c + rel % 2) % 2) for rel in (1, 2, 3)]


def greet(devices):
    barrier = pltpu.get_barrier_semaphore()
    for device in devices:
        pl.semaphore_signal(barrier, inc=1, device_id=device, device_id_type=MESH)


def await_greetings(count):
    pl.semaphore_wait(pltpu.get_barrier_semaphore(), count)


def near_mask(near, counts, width):
    blocks, listed = near.shape
    row = lax.broadcasted_iota(jnp.int32, (blocks, blocks), 0)
    own = row == lax.broadcasted_iota(jnp.int32, (blocks, blocks), 1)
    counts = jnp.sum(jnp.where(own, jnp.broadcast_to(counts, (blocks, blocks)), 0), axis=1, keepdims=True)
    lanes = lax.broadcasted_iota(jnp.int32, (blocks, width), 1)
    mask = jnp.zeros((blocks, width), F32)
    for n in range(listed):
        hit = jnp.where(near[:, n : n + 1] == lanes, 1.0, 0.0)
        mask = mask + jnp.where(counts > n, hit, 0.0)
    return mask


def pair_list(place, row_mask, col_mask):
    z, h, c, x, ny = place.z, place.h, place.c, place.x, place.ny
    sources_x = SOURCES_Y + ny
    rows, cols = row_mask.shape[0], col_mask.shape[0]
    own = rows + cols
    lane = lax.broadcasted_iota(jnp.int32, (128, 128), 0)
    k = lax.broadcasted_iota(jnp.int32, (128, 128), 1)
    rel = k // 4
    from_row = (k // 4) * (NZ * 4) + z * 4 + k % 4
    from_col = x * 16 + ((rel // 2 + h) % 2) * 8 + ((rel + c) % 2) * 4 + k % 4
    bf = jnp.bfloat16
    pick_row = jnp.where((lane == from_row) & (k < ny * 4), 1.0, 0.0).astype(bf)
    pick_col = jnp.where((lane == from_col) & (k < 16), 1.0, 0.0).astype(bf)
    dot = functools.partial(jnp.dot, preferred_element_type=F32)
    live = jnp.concatenate([dot(row_mask.astype(bf), pick_row), dot(col_mask.astype(bf), pick_col)], axis=0)
    before = dot(live.astype(bf), jnp.where(lane < k, 1.0, 0.0).astype(bf))
    totals = jnp.broadcast_to(jnp.sum(live, axis=1, keepdims=True), (own, 128))
    one = lax.broadcasted_iota(jnp.int32, (own, own), 0)
    other = lax.broadcasted_iota(jnp.int32, (own, own), 1)
    above = (one > other) & ((one < rows) | (other >= rows))
    offset = dot(jnp.where(above, 1.0, 0.0).astype(bf), totals.astype(bf))
    first = jnp.where(lax.broadcasted_iota(jnp.int32, (own, 128), 0) < rows, 0.0, 128.0 * COLS_AT)
    rank = jnp.where(live > 0.5, before + offset + first, -1.0)

    a = lax.broadcasted_iota(jnp.int32, (own, 128), 0)
    k = lax.broadcasted_iota(jnp.int32, (own, 128), 1)
    rel = k // 4
    unit = jnp.where(
        rel == 0, z, jnp.where(rel == 1, SIBLING, jnp.where(rel == 2, AHEAD + z % HALF, SIBLING + 1))
    )
    is_row = a < rows
    own_block = jnp.where(is_row, a, a - rows + sources_x * 4)
    far_block = jnp.where(is_row, SOURCES_Y * 4 + k, unit * 4 + k % 4)
    far_slot = jnp.where(is_row, k, ny * 4 + k)
    code = (own_block + 128 * far_block + 16384 * far_slot).astype(F32)

    fill = jnp.zeros((128 - own, 128), F32)
    rank_t = jnp.transpose(jnp.concatenate([rank, fill - 1.0], axis=0))[:16]
    code_t = jnp.transpose(jnp.concatenate([code, fill], axis=0))[:16]
    slots = lax.broadcasted_iota(jnp.int32, (16, 128), 1).astype(F32)
    packed = [jnp.zeros((16, 128), F32) for _ in range(MAX_PAIRS_ROWS)]
    for one in range(own):
        rank_one = jnp.broadcast_to(rank_t[:, one : one + 1], (16, 128))
        code_one = jnp.broadcast_to(code_t[:, one : one + 1], (16, 128))
        for r in range(MAX_PAIRS_ROWS):
            packed[r] = packed[r] + jnp.where(rank_one == slots + 128.0 * r, code_one, 0.0)
    listing = [jnp.sum(part, axis=0, keepdims=True) for part in packed]
    counts = [jnp.sum(part, axis=0, keepdims=True) for part in (totals[:rows], totals[rows:])]
    return jnp.concatenate(listing + counts, axis=0).astype(jnp.int32)


def gather_kernel(
    nx,
    ny,
    source_ref,
    adjoint_ref,
    points_hbm,
    near_rows_hbm,
    counts_rows_hbm,
    near_cols_hbm,
    counts_cols_hbm,
    blocks_ref,
    own_axes_ref,
    far_axes_ref,
    list_ref,
    points_ref,
    near_rows_ref,
    counts_rows_ref,
    near_cols_ref,
    counts_cols_ref,
    own_meta,
    meta_ref,
    through_send,
    through_recv,
    extra_send,
    extra_recv,
    core_send,
    core_recv,
    y_send,
    y_recv,
    x_send,
    x_recv,
    meta_send,
    meta_recv,
    local_sem,
    small_sem,
):
    smalls = [
        pltpu.make_async_copy(src, dst, small_sem.at[i])
        for i, (src, dst) in enumerate(
            (
                (points_hbm, points_ref),
                (near_rows_hbm, near_rows_ref),
                (counts_rows_hbm, counts_rows_ref),
                (near_cols_hbm, near_cols_ref),
                (counts_cols_hbm, counts_cols_ref),
            )
        )
    ]
    for copy in smalls:
        copy.start()
    place = Place(nx, ny)
    z, x, y = place.z, place.x, place.y
    per_device = source_ref.shape[0]
    sources_x = SOURCES_Y + ny
    right, left = place.beside(True), place.beside(False)
    sides = (right, left)
    others_z, others_y, others_x, others_hc = (
        place.others_z(),
        place.others_y(),
        place.others_x(),
        place.others_hc(),
    )
    sibling = others_hc[0]
    met = [device for _, device in others_z] + others_y + [device for _, device in others_x] + others_hc
    met = met + [right, left]
    greet(met)

    for copy in smalls:
        copy.wait()
    points = points_ref[...].astype(F32).reshape(3 * per_device, 128)
    row_mask = near_mask(near_rows_ref[...], counts_rows_ref[...], 128)
    col_mask = near_mask(near_cols_ref[...], counts_cols_ref[...], 128)
    for which, mask in enumerate((row_mask, col_mask)):
        own_meta[which] = jnp.concatenate([points, mask], axis=0).astype(jnp.bfloat16)

    await_greetings(len(met))

    def remote(src, dst, send, recv, device):
        return pltpu.make_async_remote_copy(
            src_ref=src, dst_ref=dst, send_sem=send, recv_sem=recv, device_id=device, device_id_type=MESH
        )

    chunks = per_device * SPLIT
    depth = source_ref.shape[1] // SPLIT
    hop = 3 * chunks // 4

    def part(ref, s):
        return ref.at[s // SPLIT, pl.ds(s % SPLIT * depth, depth)]

    def mirrored(side):
        return z if side == 0 else NZ - 1 - z

    def slot_of(side, unit):
        return unit if side == 0 else NZ - 1 - unit

    def through_unit(side, m, t):
        near = jnp.where(m < HALF, m - 1 - t, HALF - 1 - t)
        ahead = HALF - 1 - (t - m)
        is_near = (m >= HALF) | (t < m)
        return jnp.where(is_near, slot_of(side, near), AHEAD + (ahead if side == 0 else HALF - 1 - ahead))

    def passes_on(m, t):
        return (m >= HALF) | (t < HALF - 1)

    def through_copy(side, t, b):
        m = mirrored(side)
        unit = through_unit(side, m, t)
        crossed = AHEAD + unit if side == 0 else AHEAD + unit - HALF
        return remote(
            part(blocks_ref.at[unit], b),
            part(blocks_ref.at[jnp.where(m == NZ - 1, crossed, unit)], b),
            through_send.at[side, t + 1, b],
            through_recv.at[side, jnp.where(m < HALF, t + 1, t), b],
            sides[side],
        )

    def through_arrival(side, t, b):
        slot = part(blocks_ref.at[through_unit(side, mirrored(side), t)], b)
        return remote(slot, slot, through_send.at[side, t + 1, b], through_recv.at[side, t, b], sides[side])

    def extra_copy(side, e, b):
        slot = part(blocks_ref.at[slot_of(side, mirrored(side) - 1 - e)], b)
        return remote(slot, slot, extra_send.at[side, e + 1, b], extra_recv.at[side, e + 1, b], sides[side])

    def extra_arrival(side, e, b):
        slot = part(blocks_ref.at[slot_of(side, mirrored(side) - 1 - e)], b)
        return remote(slot, slot, extra_send.at[side, e + 1, b], extra_recv.at[side, e, b], sides[side])

    def own_copy(side, b):
        send, recv = through_send.at[side, 0, b], through_recv.at[side, 0, b]
        return remote(part(adjoint_ref, b), part(blocks_ref.at[z], b), send, recv, sides[side])

    def own_extra_copy(side, b):
        send, recv = extra_send.at[side, 0, b], extra_recv.at[side, 0, b]
        return remote(part(adjoint_ref, b), part(blocks_ref.at[z], b), send, recv, sides[side])

    def sends_extra(m):
        return (m >= HALF) & (m < NZ - 1)

    def core_copy(b):
        return remote(
            part(blocks_ref.at[AHEAD + z % HALF], b),
            part(blocks_ref.at[SIBLING + 1], b),
            core_send.at[b],
            core_recv.at[b],
            sibling,
        )

    core_own = remote(
        adjoint_ref, blocks_ref.at[SIBLING], core_send.at[chunks], core_recv.at[chunks], sibling
    )

    for b in range(chunks):
        for side in (0, 1):
            m = mirrored(side)

            @pl.when(m < HALF)
            def _():
                own_copy(side, b).start()

            @pl.when(sends_extra(m) & ((m > HALF) | (b < hop)))
            def _():
                own_extra_copy(side, b).start()

    metas = []
    own_slots = [z, NZ + x, NZ + nx + y, NZ + nx + ny]
    for d, (_, device) in enumerate(others_z):
        metas.append((0, own_slots[0], d, device, (z + NZ - 1 - d) % NZ))
    for d, (_, device) in enumerate(others_x):
        metas.append((1, own_slots[1], NZ + d, device, NZ + (x + nx - 1 - d) % nx))
    for d, device in enumerate(others_y):
        metas.append((1, own_slots[2], NZ + nx + d, device, NZ + nx + (y + ny - 1 - d) % ny))
    for d, device in enumerate(others_hc):
        metas.append((1, NZ + nx + ny + 1 + d, NZ + nx + ny + d, device, NZ + nx + ny + 1 + d))
    meta_out = [
        remote(own_meta.at[which], meta_ref.at[slot], meta_send.at[s], meta_recv.at[s], device)
        for which, slot, s, device, _ in metas
    ]
    meta_in = [
        remote(own_meta.at[which], meta_ref.at[slot], meta_send.at[s], meta_recv.at[s], device)
        for which, _, s, device, slot in metas
    ]
    for copy in meta_out:
        copy.start()
    core_own.start()
    y_out, y_in, x_out, x_in = [], [], [], []
    for d, device in enumerate(others_y):
        sems = (y_send.at[d], y_recv.at[d], device)
        y_out.append(remote(source_ref, blocks_ref.at[SOURCES_Y + y], *sems))
        y_in.append(remote(source_ref, blocks_ref.at[SOURCES_Y + (y + ny - 1 - d) % ny], *sems))
    for d, (_, device) in enumerate(others_x):
        sems = (x_send.at[d], x_recv.at[d], device)
        x_out.append(remote(source_ref, blocks_ref.at[sources_x + x], *sems))
        x_in.append(remote(source_ref, blocks_ref.at[sources_x + (x + nx - 1 - d) % nx], *sems))
    for copy in y_out + x_out:
        copy.start()
    locals_ = [
        pltpu.make_async_copy(adjoint_ref, blocks_ref.at[z], local_sem.at[0]),
        pltpu.make_async_copy(source_ref, blocks_ref.at[SOURCES_Y + y], local_sem.at[1]),
        pltpu.make_async_copy(source_ref, blocks_ref.at[sources_x + x], local_sem.at[2]),
    ]
    for copy in locals_:
        copy.start()
    for which, slot in zip((0, 1, 1, 1), own_slots):
        meta_ref[slot] = own_meta[which]

    def ring_step(s, carry):
        for side in (0, 1):
            m = mirrored(side)
            far = s - hop * (m - HALF + 1)
            near = s - hop
            ahead = s - hop * (HALF + 1) + (chunks - hop) * m
            is_near = near < chunks * m
            q = jnp.where(m >= HALF, far, jnp.where(is_near, near, ahead))
            comes = (q >= 0) & (q < HALF * chunks) & ((m >= HALF) | is_near | (ahead >= chunks * m))
            t, b = jnp.maximum(q, 0) // chunks, jnp.maximum(q, 0) % chunks

            @pl.when(comes)
            def _():
                through_arrival(side, t, b).wait_recv()

                @pl.when(passes_on(m, t))
                def _():
                    through_copy(side, t, b).start()

                @pl.when((m < HALF) & (t == HALF - 1))
                def _():
                    core_copy(b).start()

            late = far - HALF * chunks
            is_late = (m > HALF) & (m < NZ - 1) & (late >= 0) & (late < chunks)
            is_early = (m == NZ - 2) & (near >= 0) & (near < chunks)

            @pl.when(is_late | is_early)
            def _():
                e = jnp.where(is_late & (m == NZ - 2), 1, 0)
                b = jnp.where(is_late, late, near)
                extra_arrival(side, e, b).wait_recv()
                extra_copy(side, e, b).start()

            @pl.when((m == HALF) & (late == 0))
            def _():
                for b in range(hop, chunks):
                    own_extra_copy(side, b).start()

        return carry

    slots = (HALF + 1) * hop + HALF * chunks
    fars = far_axes_ref.shape[0]
    first_far = NZ + nx
    each = -(-fars // (slots - MET_AT - 1))
    at_end = (z == 0) | (z == NZ - 1)
    listed_at = jnp.where(at_end, LISTED_AT[0], LISTED_AT[1])
    axis = lax.broadcasted_iota(jnp.int32, (4 * per_device, 3 * 128), 0)
    wanted = lax.broadcasted_iota(jnp.int32, (4 * per_device, 3 * 128), 1) // 128 * per_device

    def spread_far(j):
        spread = jnp.where(axis == wanted + j % per_device, 1.0, 0.0).astype(jnp.bfloat16)
        far_axes_ref[j] = lax.dot_general(
            meta_ref[first_far + j // per_device], spread, (((0,), (0,)), ((), ())), preferred_element_type=F32
        )

    def list_pairs():
        masks = [meta_ref[u].astype(F32)[3 * per_device :] for u in range(NZ + nx)]
        row_masks = jnp.concatenate(masks[:NZ], axis=0)
        col_masks = jnp.concatenate(masks[NZ:], axis=0)
        list_ref[...] = pair_list(place, row_masks, col_masks)
        for u in range(NZ + nx):
            tile = meta_ref[u].astype(F32)
            for b in range(per_device):
                for c in range(3):
                    row = c * per_device + b
                    own_axes_ref[u * per_device + b, c : c + 1, :] = tile[row : row + 1]

    def ring_and_more(s, carry):
        ring_step(s, carry)

        @pl.when(s == MET_AT)
        def _():
            for copy in meta_in:
                copy.wait_recv()

        @pl.when(s == listed_at)
        def _():
            list_pairs()

        for e in range(each):
            j = (s - MET_AT - 1) * each + e

            @pl.when((j >= 0) & (j < fars))
            def _():
                spread_far(j)

        return carry

    lax.fori_loop(hop, slots, ring_and_more, 0)

    for side in (0, 1):

        @pl.when(mirrored(side) == NZ - 1)
        def _():
            def kept(s, carry):
                extra_arrival(side, s // chunks, s % chunks).wait_recv()
                return carry

            lax.fori_loop(0, (HALF - 1) * chunks, kept, 0)


    for copy in y_in + x_in:
        copy.wait_recv()
    for b in range(chunks):
        core_copy(b).wait_recv()
    core_own.wait_recv()
    for copy in locals_:
        copy.wait()
    for copy in y_out + x_out + meta_out + [core_own]:
        copy.wait_send()
    def sent(b, carry):
        core_copy(b).wait_send()
        for side in (0, 1):
            m = mirrored(side)

            @pl.when(m < HALF)
            def _():
                own_copy(side, b).wait_send()

            @pl.when(sends_extra(m))
            def _():
                own_extra_copy(side, b).wait_send()

            for t in range(HALF):

                @pl.when(passes_on(m, t))
                def _():
                    through_copy(side, t, b).wait_send()

            for e in range(2):

                @pl.when((m > HALF + e) & (m < NZ - 1))
                def _():
                    extra_copy(side, e, b).wait_send()

        return carry

    lax.fori_loop(0, chunks, sent, 0)


UNROLL = 8
STATIC_ROWS = 64
STATIC_COLS = 40


def decode(code, rows, shift):
    own_block = code & 127
    return own_block, (code >> 7) & 127, code >> 14, jnp.where(own_block < rows, own_block, own_block - shift)


def pair_term(blocks, own_axes_ref, far_axes, entry):
    own_block, far_block, far_slot, acc_slot = entry
    weights = lax.dot_general(
        blocks[far_block], blocks[own_block], (((1,), (1,)), ((), ())), preferred_element_type=F32
    )
    tile = own_axes_ref[acc_slot]
    own_axes = [jnp.broadcast_to(tile[c : c + 1], (8, 128)) for c in range(3)]
    sums = [jnp.zeros((8, 128), F32) for _ in range(3)]
    for r in range(16):
        at = slice(8 * r, 8 * r + 8)
        d = [far_axes[far_slot, at, 128 * c : 128 * c + 128] - own_axes[c] for c in range(3)]
        inverse = lax.rsqrt(d[0] * d[0] + d[1] * d[1] + d[2] * d[2] + EPS2)
        scaled = weights[at] * (inverse * inverse * inverse)
        sums = [sums[c] + d[c] * scaled for c in range(3)]
    return sums


def pair_kernel(rows, own, shift, list_ref, blocks, own_axes_ref, far_axes, out_ref, acc):
    per_device = out_ref.shape[1] // 4
    out_ref[...] = jnp.zeros_like(out_ref)
    kinds = []
    for kind, (first, done) in enumerate(((0, STATIC_ROWS), (COLS_AT, STATIC_COLS))):
        kinds.append((first, done, list_ref[MAX_PAIRS_ROWS + kind, 0]))

    @pl.when((kinds[0][2] > STATIC_ROWS) | (kinds[1][2] > STATIC_COLS))
    def _():
        acc[...] = jnp.zeros_like(acc)
        for first, done, count in kinds:

            def step(i, carry):
                for u in range(UNROLL):
                    k = i * UNROLL + u
                    entry = decode(list_ref[first + k // 128, k % 128], rows, shift)
                    sums = pair_term(blocks, own_axes_ref, far_axes, entry)
                    slot = jnp.where(k < count, entry[3], own)
                    for c in range(3):
                        acc[slot, c] = acc[slot, c] + sums[c]
                return carry

            lax.fori_loop(done // UNROLL, (count + UNROLL - 1) // UNROLL, step, 0)
        for a in range(own):
            for c in range(3):
                row = c * per_device + a % per_device
                out_ref[a // per_device, row : row + 1, :] = jnp.sum(acc[a, c], axis=0, keepdims=True)


def sums_kernel(
    nx,
    ny,
    rows,
    own,
    shift,
    list_ref,
    listing_ref,
    blocks,
    own_axes_ref,
    far_axes,
    rest_ref,
    out_ref,
    terms,
    parts_ref,
    landed,
    send_sem,
    recv_sem,
):
    place = Place(nx, ny)
    z, x = place.z, place.x
    others_z, others_x = place.others_z(), place.others_x()
    met = [device for _, device in others_z] + [device for _, device in others_x]
    greet(met)
    per_device = out_ref.shape[1]

    terms[...] = jnp.zeros_like(terms)
    k = lax.broadcasted_iota(jnp.int32, (own, 128), 1)
    owner = lax.broadcasted_iota(jnp.int32, (own, 128), 0)

    def static_pairs(kind, first, length, units):
        def step(i, carry):
            done = []
            for u in range(UNROLL):
                entry = decode(list_ref[first, i * UNROLL + u], rows, shift)
                sums = pair_term(blocks, own_axes_ref, far_axes, entry)
                done.append(jnp.concatenate([jnp.sum(part, axis=0, keepdims=True) for part in sums], axis=1))
            terms[pl.ds(pl.multiple_of(i * UNROLL, UNROLL), UNROLL), :] = jnp.concatenate(done, axis=0)
            return carry

        lax.fori_loop(0, length // UNROLL, step, 0)
        codes = jnp.broadcast_to(listing_ref[first : first + 1, :], (own, 128))
        at = MAX_PAIRS_ROWS + kind
        count = jnp.broadcast_to(listing_ref[at : at + 1, :], (own, 128))
        mine = (decode(codes, rows, shift)[3] == owner) & (k < count) & (k < length)
        owns = jnp.where(mine, 1.0, 0.0)
        acc = jnp.dot(owns, terms[...], preferred_element_type=F32, precision=lax.Precision.HIGHEST)
        for u in units:
            for c in range(3):
                at = slice(c * per_device, (c + 1) * per_device)
                parts_ref[u, at, :] = (
                    rest_ref[u, at, :] + acc[u * per_device : (u + 1) * per_device, 128 * c : 128 * c + 128]
                )

    outgoing, incoming = [], []

    def both(s, theirs, mine, source, device):
        for slot, copies in ((mine, outgoing), (source, incoming)):
            copies.append(
                pltpu.make_async_remote_copy(
                    src_ref=parts_ref.at[theirs],
                    dst_ref=landed.at[slot],
                    send_sem=send_sem.at[s],
                    recv_sem=recv_sem.at[s],
                    device_id=device,
                    device_id_type=MESH,
                )
            )

    for d, (other, device) in enumerate(others_z):
        both(d, other, z, (z + NZ - 1 - d) % NZ, device)
    for d, (other, device) in enumerate(others_x):
        both(NZ + d, NZ + other, NZ + x, NZ + (x + nx - 1 - d) % nx, device)

    static_pairs(0, 0, STATIC_ROWS, range(NZ))
    await_greetings(len(met))
    for copy in outgoing[: NZ - 1]:
        copy.start()
    static_pairs(1, COLS_AT, STATIC_COLS, range(NZ, NZ + nx))
    for copy in outgoing[NZ - 1 :]:
        copy.start()
    landed[z] = parts_ref[z]
    landed[NZ + x] = parts_ref[NZ + x]
    for copy in incoming:
        copy.wait_recv()
    total = landed[0]
    for u in range(1, NZ + nx):
        total = total + landed[u]
    for c in range(3):
        out_ref[c] = total[c * per_device : (c + 1) * per_device]
    for copy in outgoing:
        copy.wait_send()


def shards(
    nx,
    ny,
    source_strength,
    adjoint_strength,
    node_points,
    near_rows,
    counts_rows,
    near_cols,
    counts_cols,
):
    _, per_device, size_block, conditions = source_strength.shape
    units = SOURCES_Y + ny + nx
    metas = NZ + nx + ny + 4
    dma = pltpu.SemaphoreType.DMA
    any_space = pl.BlockSpec(memory_space=pl.ANY)
    hbm = pl.BlockSpec(memory_space=pltpu.HBM)
    fars = (ny + 4) * per_device
    small = pltpu.CompilerParams(vmem_limit_bytes=8 * 1024 * 1024)
    vmem = pl.BlockSpec(memory_space=pltpu.VMEM)
    blocks, own_axes, far_axes, listing = pl.pallas_call(
        functools.partial(gather_kernel, nx, ny),
        name="gather",
        out_shape=(
            jax.ShapeDtypeStruct((units, per_device, size_block, conditions), jnp.bfloat16),
            jax.ShapeDtypeStruct(((NZ + nx) * per_device, 8, 128), F32),
            jax.ShapeDtypeStruct((fars, size_block, 3 * 128), F32),
            jax.ShapeDtypeStruct((8, 128), jnp.int32),
        ),
        in_specs=[hbm] * 7,
        out_specs=(any_space, vmem, vmem, vmem),
        scratch_shapes=[
            pltpu.VMEM((3, per_device, size_block), jnp.bfloat16),
            pltpu.VMEM((per_device, near_rows.shape[2]), jnp.int32),
            pltpu.VMEM((1, per_device), jnp.int32),
            pltpu.VMEM((per_device, near_cols.shape[2]), jnp.int32),
            pltpu.VMEM((1, per_device), jnp.int32),
            pltpu.VMEM((2, 4 * per_device, 128), jnp.bfloat16),
            pltpu.VMEM((metas, 4 * per_device, 128), jnp.bfloat16),
            dma((2, HALF + 1, per_device * SPLIT)),
            dma((2, HALF, per_device * SPLIT)),
            dma((2, HALF, per_device * SPLIT)),
            dma((2, HALF, per_device * SPLIT)),
            dma((per_device * SPLIT + 1,)),
            dma((per_device * SPLIT + 1,)),
            dma((max(ny - 1, 1),)),
            dma((max(ny - 1, 1),)),
            dma((max(nx - 1, 1),)),
            dma((max(nx - 1, 1),)),
            dma((metas,)),
            dma((metas,)),
            dma((3,)),
            dma((5,)),
        ],
        compiler_params=pltpu.CompilerParams(
            collective_id=0, has_side_effects=True, vmem_limit_bytes=16 * 1024 * 1024
        ),
    )(
        *(
            pltpu.with_memory_space_constraint(operand, pltpu.HBM)
            for operand in (
                source_strength[0],
                adjoint_strength[0],
                jnp.transpose(node_points[0], (1, 0, 2)),
                near_rows[0],
                counts_rows,
                near_cols[0],
                counts_cols,
            )
        )
    )
    rows = NZ * per_device
    own = rows + nx * per_device
    shift = (SOURCES_Y + ny) * per_device - rows
    blocks = blocks.reshape(units * per_device, size_block, conditions)
    smem = pl.BlockSpec(memory_space=pltpu.SMEM)
    parts_shape = (NZ + nx, 4 * per_device, 128)
    rest = pl.pallas_call(
        functools.partial(pair_kernel, rows, own, shift),
        name="pairs",
        out_shape=jax.ShapeDtypeStruct(parts_shape, F32),
        in_specs=[smem, vmem, vmem, vmem],
        out_specs=vmem,
        scratch_shapes=[pltpu.VMEM((own + 1, 3, 8, 128), F32)],
        compiler_params=small,
    )(listing, blocks, own_axes, far_axes)
    total = pl.pallas_call(
        functools.partial(sums_kernel, nx, ny, rows, own, shift),
        name="sums",
        out_shape=jax.ShapeDtypeStruct((3, per_device, 128), F32),
        in_specs=[smem] + [vmem] * 5,
        out_specs=vmem,
        scratch_shapes=[
            pltpu.VMEM((128, 3 * 128), F32),
            pltpu.VMEM(parts_shape, F32),
            pltpu.VMEM(parts_shape, F32),
            dma((NZ + nx,)),
            dma((NZ + nx,)),
        ],
        compiler_params=pltpu.CompilerParams(
            collective_id=1, has_side_effects=True, vmem_limit_bytes=8 * 1024 * 1024
        ),
    )(listing, listing, blocks, own_axes, far_axes, rest)
    return jnp.transpose(total, (1, 0, 2))[None]


def solution(mesh):
    nx, ny = mesh.shape["blk"] // 4, mesh.shape["wide"] // NZ
    return jax.shard_map(
        functools.partial(shards, nx, ny),
        mesh=mesh,
        in_specs=(
            P("blk", "wide", None, None),
            P("blk", "wide", None, None),
            P("blk", "wide", None, None),
            P("blk", "wide", None),
            P("blk", "wide"),
            P("blk", "wide", None),
            P("blk", "wide"),
        ),
        out_specs=P("blk", "wide", None, None),
        check_vma=False,
    )
```

```python
import functools

import jax
import jax.numpy as jnp
from jax import lax
from jax.experimental import pallas as pl
from jax.experimental.pallas import tpu as pltpu
from jax.sharding import PartitionSpec as P

EPS2 = 0.04
MESH = pl.DeviceIdType.MESH
F32 = jnp.float32

NZ = 8
HALF = NZ // 2
AHEAD = NZ
SOURCES_Y = AHEAD + HALF
COLS_AT = 4
MAX_PAIRS_ROWS = 6
SPLIT = 1
MET_AT = 8
LISTED_AT = 28, 28


class Place:
    def __init__(self, nx, ny):
        self.nx, self.ny = nx, ny
        self.wide, self.blk = lax.axis_index("wide"), lax.axis_index("blk")
        self.y, self.z = self.wide // NZ, self.wide % NZ
        self.x, self.h, self.c = self.blk // 4, (self.blk // 2) % 2, self.blk % 2

    def at(self, y=None, z=None, x=None, h=None, c=None):
        pick = lambda given, mine: mine if given is None else given
        wide = pick(y, self.y) * NZ + pick(z, self.z)
        blk = pick(x, self.x) * 4 + pick(h, self.h) * 2 + pick(c, self.c)
        return {"wide": wide, "blk": blk}

    def beside(self, right):
        if right:
            crosses = (self.z == NZ - 1).astype(jnp.int32)
            z = (self.z + 1) % NZ
        else:
            crosses = (self.z == 0).astype(jnp.int32)
            z = (self.z + NZ - 1) % NZ
        return self.at(z=z, h=(self.h + crosses) % 2)

    def others_z(self):
        return [((self.z + d) % NZ, self.at(z=(self.z + d) % NZ)) for d in range(1, NZ)]

    def others_y(self):
        return [self.at(y=(self.y + d) % self.ny) for d in range(1, self.ny)]

    def others_xc(self):
        found = []
        for d in range(1, 2 * self.nx):
            to_x, from_x = (self.x + d // 2) % self.nx, (self.x + self.nx - d // 2) % self.nx
            c = (self.c + d % 2) % 2
            found.append((to_x * 2 + c, from_x * 2 + c, self.at(x=to_x, c=c)))
        return found

    def opposite(self):
        return self.at(h=1 - self.h)


def greet(devices):
    barrier = pltpu.get_barrier_semaphore()
    for device in devices:
        pl.semaphore_signal(barrier, inc=1, device_id=device, device_id_type=MESH)


def await_greetings(count):
    pl.semaphore_wait(pltpu.get_barrier_semaphore(), count)


def near_mask(near, counts, width):
    blocks, listed = near.shape
    row = lax.broadcasted_iota(jnp.int32, (blocks, blocks), 0)
    own = row == lax.broadcasted_iota(jnp.int32, (blocks, blocks), 1)
    counts = jnp.sum(jnp.where(own, jnp.broadcast_to(counts, (blocks, blocks)), 0), axis=1, keepdims=True)
    lanes = lax.broadcasted_iota(jnp.int32, (blocks, width), 1)
    mask = jnp.zeros((blocks, width), F32)
    for n in range(listed):
        hit = jnp.where(near[:, n : n + 1] == lanes, 1.0, 0.0)
        mask = mask + jnp.where(counts > n, hit, 0.0)
    return mask


def pair_list(place, row_mask, col_mask):
    z, h, c, x, ny = place.z, place.h, place.c, place.x, place.ny
    sources_x = SOURCES_Y + ny
    rows, cols = row_mask.shape[0], col_mask.shape[0]
    own = rows + cols
    lane = lax.broadcasted_iota(jnp.int32, (128, 128), 0)
    k = lax.broadcasted_iota(jnp.int32, (128, 128), 1)
    from_row = (k // 4) * (NZ * 4) + z * 4 + k % 4
    from_col = x * 16 + (k // 4 + h) % 2 * 8 + c * 4 + k % 4
    bf = jnp.bfloat16
    pick_row = jnp.where((lane == from_row) & (k < ny * 4), 1.0, 0.0).astype(bf)
    pick_col = jnp.where((lane == from_col) & (k < 8), 1.0, 0.0).astype(bf)
    dot = functools.partial(jnp.dot, preferred_element_type=F32)
    live = jnp.concatenate([dot(row_mask.astype(bf), pick_row), dot(col_mask.astype(bf), pick_col)], axis=0)
    before = dot(live.astype(bf), jnp.where(lane < k, 1.0, 0.0).astype(bf))
    totals = jnp.broadcast_to(jnp.sum(live, axis=1, keepdims=True), (own, 128))
    one = lax.broadcasted_iota(jnp.int32, (own, own), 0)
    other = lax.broadcasted_iota(jnp.int32, (own, own), 1)
    above = (one > other) & ((one < rows) | (other >= rows))
    offset = dot(jnp.where(above, 1.0, 0.0).astype(bf), totals.astype(bf))
    first = jnp.where(lax.broadcasted_iota(jnp.int32, (own, 128), 0) < rows, 0.0, 128.0 * COLS_AT)
    rank = jnp.where(live > 0.5, before + offset + first, -1.0)

    a = lax.broadcasted_iota(jnp.int32, (own, 128), 0)
    k = lax.broadcasted_iota(jnp.int32, (own, 128), 1)
    unit = jnp.where(k // 4 == 0, z, AHEAD + z % HALF)
    is_row = a < rows
    own_block = jnp.where(is_row, a, a - rows + sources_x * 4)
    far_block = jnp.where(is_row, SOURCES_Y * 4 + k, unit * 4 + k % 4)
    far_slot = jnp.where(is_row, k, ny * 4 + k)
    code = (own_block + 128 * far_block + 16384 * far_slot).astype(F32)

    fill = jnp.zeros((128 - own, 128), F32)
    rank_t = jnp.transpose(jnp.concatenate([rank, fill - 1.0], axis=0))[:16]
    code_t = jnp.transpose(jnp.concatenate([code, fill], axis=0))[:16]
    slots = lax.broadcasted_iota(jnp.int32, (16, 128), 1).astype(F32)
    packed = [jnp.zeros((16, 128), F32) for _ in range(MAX_PAIRS_ROWS)]
    for one in range(own):
        rank_one = jnp.broadcast_to(rank_t[:, one : one + 1], (16, 128))
        code_one = jnp.broadcast_to(code_t[:, one : one + 1], (16, 128))
        for r in range(MAX_PAIRS_ROWS):
            packed[r] = packed[r] + jnp.where(rank_one == slots + 128.0 * r, code_one, 0.0)
    listing = [jnp.sum(part, axis=0, keepdims=True) for part in packed]
    counts = [jnp.sum(part, axis=0, keepdims=True) for part in (totals[:rows], totals[rows:])]
    return jnp.concatenate(listing + counts, axis=0).astype(jnp.int32)


def gather_kernel(
    nx,
    ny,
    source_ref,
    adjoint_ref,
    points_hbm,
    near_rows_hbm,
    counts_rows_hbm,
    near_cols_hbm,
    counts_cols_hbm,
    blocks_ref,
    own_axes_ref,
    far_axes_ref,
    list_ref,
    points_ref,
    near_rows_ref,
    counts_rows_ref,
    near_cols_ref,
    counts_cols_ref,
    own_meta,
    meta_ref,
    through_send,
    through_recv,
    extra_send,
    extra_recv,
    y_send,
    y_recv,
    x_send,
    x_recv,
    meta_send,
    meta_recv,
    local_sem,
    small_sem,
):
    smalls = [
        pltpu.make_async_copy(src, dst, small_sem.at[i])
        for i, (src, dst) in enumerate(
            (
                (points_hbm, points_ref),
                (near_rows_hbm, near_rows_ref),
                (counts_rows_hbm, counts_rows_ref),
                (near_cols_hbm, near_cols_ref),
                (counts_cols_hbm, counts_cols_ref),
            )
        )
    ]
    for copy in smalls:
        copy.start()
    place = Place(nx, ny)
    z, x, y = place.z, place.x, place.y
    per_device = source_ref.shape[0]
    sources_x = SOURCES_Y + ny
    right, left = place.beside(True), place.beside(False)
    sides = (right, left)
    others_z, others_y, others_xc = place.others_z(), place.others_y(), place.others_xc()
    opposite = place.opposite()
    met = [device for _, device in others_z] + others_y + [device for _, _, device in others_xc]
    met = met + [opposite, right, left]
    greet(met)

    for copy in smalls:
        copy.wait()
    points = points_ref[...].astype(F32).reshape(3 * per_device, 128)
    row_mask = near_mask(near_rows_ref[...], counts_rows_ref[...], 128)
    col_mask = near_mask(near_cols_ref[...], counts_cols_ref[...], 128)
    for which, mask in enumerate((row_mask, col_mask)):
        own_meta[which] = jnp.concatenate([points, mask], axis=0).astype(jnp.bfloat16)

    await_greetings(len(met))

    def remote(src, dst, send, recv, device):
        return pltpu.make_async_remote_copy(
            src_ref=src, dst_ref=dst, send_sem=send, recv_sem=recv, device_id=device, device_id_type=MESH
        )

    chunks = per_device * SPLIT
    depth = source_ref.shape[1] // SPLIT
    hop = 3 * chunks // 4

    def part(ref, s):
        return ref.at[s // SPLIT, pl.ds(s % SPLIT * depth, depth)]

    def mirrored(side):
        return z if side == 0 else NZ - 1 - z

    def slot_of(side, unit):
        return unit if side == 0 else NZ - 1 - unit

    def through_unit(side, m, t):
        near = jnp.where(m < HALF, m - 1 - t, HALF - 1 - t)
        ahead = HALF - 1 - (t - m)
        is_near = (m >= HALF) | (t < m)
        return jnp.where(is_near, slot_of(side, near), AHEAD + (ahead if side == 0 else HALF - 1 - ahead))

    def passes_on(m, t):
        return (m >= HALF) | (t < HALF - 1)

    def through_copy(side, t, b):
        m = mirrored(side)
        unit = through_unit(side, m, t)
        crossed = AHEAD + unit if side == 0 else AHEAD + unit - HALF
        return remote(
            part(blocks_ref.at[unit], b),
            part(blocks_ref.at[jnp.where(m == NZ - 1, crossed, unit)], b),
            through_send.at[side, t + 1],
            through_recv.at[side, jnp.where(m < HALF, t + 1, t), b],
            sides[side],
        )

    def through_arrival(side, t, b):
        slot = part(blocks_ref.at[through_unit(side, mirrored(side), t)], b)
        return remote(slot, slot, through_send.at[side, t + 1], through_recv.at[side, t, b], sides[side])

    def extra_copy(side, e, b):
        slot = part(blocks_ref.at[slot_of(side, mirrored(side) - 1 - e)], b)
        return remote(slot, slot, extra_send.at[side, e + 1], extra_recv.at[side, e + 1, b], sides[side])

    def extra_arrival(side, e, b):
        slot = part(blocks_ref.at[slot_of(side, mirrored(side) - 1 - e)], b)
        return remote(slot, slot, extra_send.at[side, e + 1], extra_recv.at[side, e, b], sides[side])

    def own_copy(side, b):
        send, recv = through_send.at[side, 0], through_recv.at[side, 0, b]
        return remote(part(adjoint_ref, b), part(blocks_ref.at[z], b), send, recv, sides[side])

    def own_extra_copy(side, b):
        send, recv = extra_send.at[side, 0], extra_recv.at[side, 0, b]
        return remote(part(adjoint_ref, b), part(blocks_ref.at[z], b), send, recv, sides[side])

    def sends_extra(m):
        return (m >= HALF) & (m < NZ - 1)

    metas = []
    mine = x * 2 + place.c
    first_y = NZ + 2 * nx
    own_slots = [z, NZ + mine, first_y + y, first_y + ny]
    for d, (_, device) in enumerate(others_z):
        metas.append((0, own_slots[0], d, device, (z + NZ - 1 - d) % NZ))
    for d, (_, source, device) in enumerate(others_xc):
        metas.append((1, own_slots[1], NZ + d, device, NZ + source))
    for d, device in enumerate(others_y):
        metas.append((1, own_slots[2], first_y + d, device, first_y + (y + ny - 1 - d) % ny))
    metas.append((1, first_y + ny + 1, first_y + ny, opposite, first_y + ny + 1))
    meta_out = [
        remote(own_meta.at[which], meta_ref.at[slot], meta_send.at[s], meta_recv.at[s], device)
        for which, slot, s, device, _ in metas
    ]
    meta_in = [
        remote(own_meta.at[which], meta_ref.at[slot], meta_send.at[s], meta_recv.at[s], device)
        for which, _, s, device, slot in metas
    ]
    for copy in meta_out:
        copy.start()
    for b in range(chunks):
        for side in (0, 1):
            m = mirrored(side)

            @pl.when(m < HALF)
            def _():
                own_copy(side, b).start()

            @pl.when(sends_extra(m) & ((m > HALF) | (b < hop)))
            def _():
                own_extra_copy(side, b).start()

    y_out, y_in, x_out, x_in = [], [], [], []
    for d, device in enumerate(others_y):
        sems = (y_send.at[d], y_recv.at[d], device)
        y_out.append(remote(source_ref, blocks_ref.at[SOURCES_Y + y], *sems))
        y_in.append(remote(source_ref, blocks_ref.at[SOURCES_Y + (y + ny - 1 - d) % ny], *sems))
    for d, (_, source, device) in enumerate(others_xc):
        sems = (x_send.at[d], x_recv.at[d], device)
        x_out.append(remote(source_ref, blocks_ref.at[sources_x + mine], *sems))
        x_in.append(remote(source_ref, blocks_ref.at[sources_x + source], *sems))
    for copy in y_out + x_out:
        copy.start()
    locals_ = [
        pltpu.make_async_copy(adjoint_ref, blocks_ref.at[z], local_sem.at[0]),
        pltpu.make_async_copy(source_ref, blocks_ref.at[SOURCES_Y + y], local_sem.at[1]),
        pltpu.make_async_copy(source_ref, blocks_ref.at[sources_x + mine], local_sem.at[2]),
    ]
    for copy in locals_:
        copy.start()
    for which, slot in zip((0, 1, 1, 1), own_slots):
        meta_ref[slot] = own_meta[which]

    def ring_step(s, carry):
        for side in (0, 1):
            m = mirrored(side)
            far = s - hop * (m - HALF + 1)
            near = s - hop
            ahead = s - hop * (HALF + 1) + (chunks - hop) * m
            is_near = near < chunks * m
            q = jnp.where(m >= HALF, far, jnp.where(is_near, near, ahead))
            comes = (q >= 0) & (q < HALF * chunks) & ((m >= HALF) | is_near | (ahead >= chunks * m))
            t, b = jnp.maximum(q, 0) // chunks, jnp.maximum(q, 0) % chunks

            @pl.when(comes)
            def _():
                through_arrival(side, t, b).wait_recv()

                @pl.when(passes_on(m, t))
                def _():
                    through_copy(side, t, b).start()

            late = far - HALF * chunks
            is_late = (m > HALF) & (m < NZ - 1) & (late >= 0) & (late < chunks)
            is_early = (m == NZ - 2) & (near >= 0) & (near < chunks)

            @pl.when(is_late | is_early)
            def _():
                e = jnp.where(is_late & (m == NZ - 2), 1, 0)
                b = jnp.where(is_late, late, near)
                extra_arrival(side, e, b).wait_recv()
                extra_copy(side, e, b).start()

            @pl.when((m == HALF) & (late == 0))
            def _():
                for b in range(hop, chunks):
                    own_extra_copy(side, b).start()

        return carry

    slots = (HALF + 1) * hop + HALF * chunks
    fars = far_axes_ref.shape[0]
    first_far = first_y
    each = -(-fars // (slots - MET_AT - 1))
    at_end = (z == 0) | (z == NZ - 1)
    listed_at = jnp.where(at_end, LISTED_AT[0], LISTED_AT[1])
    axis = lax.broadcasted_iota(jnp.int32, (4 * per_device, 3 * 128), 0)
    wanted = lax.broadcasted_iota(jnp.int32, (4 * per_device, 3 * 128), 1) // 128 * per_device

    def spread_far(j):
        spread = jnp.where(axis == wanted + j % per_device, 1.0, 0.0).astype(jnp.bfloat16)
        far_axes_ref[j] = lax.dot_general(
            meta_ref[first_far + j // per_device], spread, (((0,), (0,)), ((), ())), preferred_element_type=F32
        )

    def list_pairs():
        masks = [meta_ref[u].astype(F32)[3 * per_device :] for u in range(first_y)]
        row_masks = jnp.concatenate(masks[:NZ], axis=0)
        col_masks = jnp.concatenate(masks[NZ:], axis=0)
        list_ref[...] = pair_list(place, row_masks, col_masks)
        for u in range(first_y):
            tile = meta_ref[u].astype(F32)
            for b in range(per_device):
                for c in range(3):
                    row = c * per_device + b
                    own_axes_ref[u * per_device + b, c : c + 1, :] = tile[row : row + 1]

    def ring_and_more(s, carry):
        ring_step(s, carry)

        @pl.when(s == MET_AT)
        def _():
            for copy in meta_in:
                copy.wait_recv()

        @pl.when(s == listed_at)
        def _():
            list_pairs()

        for e in range(each):
            j = (s - MET_AT - 1) * each + e

            @pl.when((j >= 0) & (j < fars))
            def _():
                spread_far(j)

        return carry

    lax.fori_loop(hop, slots, ring_and_more, 0)

    for side in (0, 1):

        @pl.when(mirrored(side) == NZ - 1)
        def _():
            def kept(s, carry):
                extra_arrival(side, s // chunks, s % chunks).wait_recv()
                return carry

            lax.fori_loop(0, (HALF - 1) * chunks, kept, 0)


    for copy in y_in + x_in:
        copy.wait_recv()
    for copy in locals_:
        copy.wait()
    for copy in y_out + x_out + meta_out:
        copy.wait_send()
    def unit_sent(semaphore):
        remote(blocks_ref.at[z], blocks_ref.at[z], semaphore, through_recv.at[0, 0, 0], right).wait_send()

    for side in (0, 1):
        m = mirrored(side)

        @pl.when(m < HALF)
        def _():
            unit_sent(through_send.at[side, 0])

        @pl.when(sends_extra(m))
        def _():
            unit_sent(extra_send.at[side, 0])

        for t in range(HALF):

            @pl.when(passes_on(m, t))
            def _():
                unit_sent(through_send.at[side, t + 1])

        for e in range(2):

            @pl.when((m > HALF + e) & (m < NZ - 1))
            def _():
                unit_sent(extra_send.at[side, e + 1])


UNROLL = 8
STATIC_ROWS = 64
STATIC_COLS = 24


def decode(code, rows, shift):
    own_block = code & 127
    return own_block, (code >> 7) & 127, code >> 14, jnp.where(own_block < rows, own_block, own_block - shift)


def pair_term(blocks, own_axes_ref, far_axes, entry):
    own_block, far_block, far_slot, acc_slot = entry
    weights = lax.dot_general(
        blocks[far_block], blocks[own_block], (((1,), (1,)), ((), ())), preferred_element_type=F32
    )
    tile = own_axes_ref[acc_slot]
    own_axes = [jnp.broadcast_to(tile[c : c + 1], (8, 128)) for c in range(3)]
    sums = [jnp.zeros((8, 128), F32) for _ in range(3)]
    for r in range(16):
        at = slice(8 * r, 8 * r + 8)
        d = [far_axes[far_slot, at, 128 * c : 128 * c + 128] - own_axes[c] for c in range(3)]
        inverse = lax.rsqrt(d[0] * d[0] + d[1] * d[1] + d[2] * d[2] + EPS2)
        scaled = weights[at] * (inverse * inverse * inverse)
        sums = [sums[c] + d[c] * scaled for c in range(3)]
    return sums


def pair_kernel(rows, own, shift, list_ref, blocks, own_axes_ref, far_axes, out_ref, acc):
    per_device = out_ref.shape[1] // 4
    out_ref[...] = jnp.zeros_like(out_ref)
    kinds = []
    for kind, (first, done) in enumerate(((0, STATIC_ROWS), (COLS_AT, STATIC_COLS))):
        kinds.append((first, done, list_ref[MAX_PAIRS_ROWS + kind, 0]))

    @pl.when((kinds[0][2] > STATIC_ROWS) | (kinds[1][2] > STATIC_COLS))
    def _():
        acc[...] = jnp.zeros_like(acc)
        for first, done, count in kinds:

            def step(i, carry):
                for u in range(UNROLL):
                    k = i * UNROLL + u
                    entry = decode(list_ref[first + k // 128, k % 128], rows, shift)
                    sums = pair_term(blocks, own_axes_ref, far_axes, entry)
                    slot = jnp.where(k < count, entry[3], own)
                    for c in range(3):
                        acc[slot, c] = acc[slot, c] + sums[c]
                return carry

            lax.fori_loop(done // UNROLL, (count + UNROLL - 1) // UNROLL, step, 0)
        for a in range(own):
            for c in range(3):
                row = c * per_device + a % per_device
                out_ref[a // per_device, row : row + 1, :] = jnp.sum(acc[a, c], axis=0, keepdims=True)


def sums_kernel(
    nx,
    ny,
    rows,
    own,
    shift,
    list_ref,
    listing_ref,
    blocks,
    own_axes_ref,
    far_axes,
    rest_ref,
    out_ref,
    terms,
    parts_ref,
    landed,
    send_sem,
    recv_sem,
):
    place = Place(nx, ny)
    z, x = place.z, place.x
    others_z, others_xc = place.others_z(), place.others_xc()
    mine = x * 2 + place.c
    met = [device for _, device in others_z] + [device for _, _, device in others_xc]
    greet(met)
    per_device = out_ref.shape[1]

    terms[...] = jnp.zeros_like(terms)
    k = lax.broadcasted_iota(jnp.int32, (own, 128), 1)
    owner = lax.broadcasted_iota(jnp.int32, (own, 128), 0)

    def static_pairs(kind, first, length, units):
        def step(i, carry):
            done = []
            for u in range(UNROLL):
                entry = decode(list_ref[first, i * UNROLL + u], rows, shift)
                sums = pair_term(blocks, own_axes_ref, far_axes, entry)
                done.append(jnp.concatenate([jnp.sum(part, axis=0, keepdims=True) for part in sums], axis=1))
            terms[pl.ds(pl.multiple_of(i * UNROLL, UNROLL), UNROLL), :] = jnp.concatenate(done, axis=0)
            return carry

        lax.fori_loop(0, length // UNROLL, step, 0)
        codes = jnp.broadcast_to(listing_ref[first : first + 1, :], (own, 128))
        at = MAX_PAIRS_ROWS + kind
        count = jnp.broadcast_to(listing_ref[at : at + 1, :], (own, 128))
        has = (decode(codes, rows, shift)[3] == owner) & (k < count) & (k < length)
        owns = jnp.where(has, 1.0, 0.0)
        acc = jnp.dot(owns, terms[...], preferred_element_type=F32, precision=lax.Precision.HIGHEST)
        for u in units:
            for c in range(3):
                at = slice(c * per_device, (c + 1) * per_device)
                parts_ref[u, at, :] = (
                    rest_ref[u, at, :] + acc[u * per_device : (u + 1) * per_device, 128 * c : 128 * c + 128]
                )

    outgoing, incoming = [], []

    def both(s, theirs, mine, source, device):
        for slot, copies in ((mine, outgoing), (source, incoming)):
            copies.append(
                pltpu.make_async_remote_copy(
                    src_ref=parts_ref.at[theirs],
                    dst_ref=landed.at[slot],
                    send_sem=send_sem.at[s],
                    recv_sem=recv_sem.at[s],
                    device_id=device,
                    device_id_type=MESH,
                )
            )

    for d, (other, device) in enumerate(others_z):
        both(d, other, z, (z + NZ - 1 - d) % NZ, device)
    for d, (other, source, device) in enumerate(others_xc):
        both(NZ + d, NZ + other, NZ + mine, NZ + source, device)

    static_pairs(0, 0, STATIC_ROWS, range(NZ))
    await_greetings(len(met))
    for copy in outgoing[: NZ - 1][::-1]:
        copy.start()
    static_pairs(1, COLS_AT, STATIC_COLS, range(NZ, NZ + 2 * nx))
    for copy in outgoing[NZ - 1 :]:
        copy.start()
    landed[z] = parts_ref[z]
    landed[NZ + mine] = parts_ref[NZ + mine]
    for copy in incoming:
        copy.wait_recv()
    total = landed[0]
    for u in range(1, NZ + 2 * nx):
        total = total + landed[u]
    for c in range(3):
        out_ref[c] = total[c * per_device : (c + 1) * per_device]
    for copy in outgoing:
        copy.wait_send()


def shards(
    nx,
    ny,
    source_strength,
    adjoint_strength,
    node_points,
    near_rows,
    counts_rows,
    near_cols,
    counts_cols,
):
    _, per_device, size_block, conditions = source_strength.shape
    units = SOURCES_Y + ny + 2 * nx
    metas = NZ + 2 * nx + ny + 2
    dma = pltpu.SemaphoreType.DMA
    any_space = pl.BlockSpec(memory_space=pl.ANY)
    hbm = pl.BlockSpec(memory_space=pltpu.HBM)
    fars = (ny + 2) * per_device
    small = pltpu.CompilerParams(vmem_limit_bytes=8 * 1024 * 1024)
    vmem = pl.BlockSpec(memory_space=pltpu.VMEM)
    blocks, own_axes, far_axes, listing = pl.pallas_call(
        functools.partial(gather_kernel, nx, ny),
        name="gather",
        out_shape=(
            jax.ShapeDtypeStruct((units, per_device, size_block, conditions), jnp.bfloat16),
            jax.ShapeDtypeStruct(((NZ + 2 * nx) * per_device, 8, 128), F32),
            jax.ShapeDtypeStruct((fars, size_block, 3 * 128), F32),
            jax.ShapeDtypeStruct((8, 128), jnp.int32),
        ),
        in_specs=[hbm] * 7,
        out_specs=(any_space, vmem, vmem, vmem),
        scratch_shapes=[
            pltpu.VMEM((3, per_device, size_block), jnp.bfloat16),
            pltpu.VMEM((per_device, near_rows.shape[2]), jnp.int32),
            pltpu.VMEM((1, per_device), jnp.int32),
            pltpu.VMEM((per_device, near_cols.shape[2]), jnp.int32),
            pltpu.VMEM((1, per_device), jnp.int32),
            pltpu.VMEM((2, 4 * per_device, 128), jnp.bfloat16),
            pltpu.VMEM((metas, 4 * per_device, 128), jnp.bfloat16),
            dma((2, HALF + 1)),
            dma((2, HALF, per_device * SPLIT)),
            dma((2, HALF)),
            dma((2, HALF, per_device * SPLIT)),
            dma((max(ny - 1, 1),)),
            dma((max(ny - 1, 1),)),
            dma((2 * nx - 1,)),
            dma((2 * nx - 1,)),
            dma((metas,)),
            dma((metas,)),
            dma((3,)),
            dma((5,)),
        ],
        compiler_params=pltpu.CompilerParams(
            collective_id=0, has_side_effects=True, vmem_limit_bytes=16 * 1024 * 1024
        ),
    )(
        *(
            pltpu.with_memory_space_constraint(operand, pltpu.HBM)
            for operand in (
                source_strength[0],
                adjoint_strength[0],
                jnp.transpose(node_points[0], (1, 0, 2)),
                near_rows[0],
                counts_rows,
                near_cols[0],
                counts_cols,
            )
        )
    )
    rows = NZ * per_device
    own = rows + 2 * nx * per_device
    shift = (SOURCES_Y + ny) * per_device - rows
    blocks = blocks.reshape(units * per_device, size_block, conditions)
    smem = pl.BlockSpec(memory_space=pltpu.SMEM)
    parts_shape = (NZ + 2 * nx, 4 * per_device, 128)
    rest = pl.pallas_call(
        functools.partial(pair_kernel, rows, own, shift),
        name="pairs",
        out_shape=jax.ShapeDtypeStruct(parts_shape, F32),
        in_specs=[smem, vmem, vmem, vmem],
        out_specs=vmem,
        scratch_shapes=[pltpu.VMEM((own + 1, 3, 8, 128), F32)],
        compiler_params=small,
    )(listing, blocks, own_axes, far_axes)
    total = pl.pallas_call(
        functools.partial(sums_kernel, nx, ny, rows, own, shift),
        name="sums",
        out_shape=jax.ShapeDtypeStruct((3, per_device, 128), F32),
        in_specs=[smem] + [vmem] * 5,
        out_specs=vmem,
        scratch_shapes=[
            pltpu.VMEM((128, 3 * 128), F32),
            pltpu.VMEM(parts_shape, F32),
            pltpu.VMEM(parts_shape, F32),
            dma((NZ + 2 * nx,)),
            dma((NZ + 2 * nx,)),
        ],
        compiler_params=pltpu.CompilerParams(
            collective_id=1, has_side_effects=True, vmem_limit_bytes=8 * 1024 * 1024
        ),
    )(listing, listing, blocks, own_axes, far_axes, rest)
    return jnp.transpose(total, (1, 0, 2))[None]


def solution(mesh):
    nx, ny = mesh.shape["blk"] // 4, mesh.shape["wide"] // NZ
    return jax.shard_map(
        functools.partial(shards, nx, ny),
        mesh=mesh,
        in_specs=(
            P("blk", "wide", None, None),
            P("blk", "wide", None, None),
            P("blk", "wide", None, None),
            P("blk", "wide", None),
            P("blk", "wide"),
            P("blk", "wide", None),
            P("blk", "wide"),
        ),
        out_specs=P("blk", "wide", None, None),
        check_vma=False,
    )
```

```python
import functools

import jax
import jax.numpy as jnp
from jax import lax
from jax.experimental import pallas as pl
from jax.experimental.pallas import tpu as pltpu
from jax.sharding import PartitionSpec as P

EPS2 = 0.04
MESH = pl.DeviceIdType.MESH
F32 = jnp.float32

NZ = 8
HALF = NZ // 2
AHEAD = NZ
SOURCES_Y = AHEAD + HALF
COLS_AT = 4
MAX_PAIRS_ROWS = 6
SPLIT = 1
MET_AT = 8
LISTED_AT = 28, 28


class Place:
    def __init__(self, nx, ny):
        self.nx, self.ny = nx, ny
        self.wide, self.blk = lax.axis_index("wide"), lax.axis_index("blk")
        self.y, self.z = self.wide // NZ, self.wide % NZ
        self.x, self.h, self.c = self.blk // 4, (self.blk // 2) % 2, self.blk % 2

    def at(self, y=None, z=None, x=None, h=None, c=None):
        pick = lambda given, mine: mine if given is None else given
        wide = pick(y, self.y) * NZ + pick(z, self.z)
        blk = pick(x, self.x) * 4 + pick(h, self.h) * 2 + pick(c, self.c)
        return {"wide": wide, "blk": blk}

    def beside(self, right):
        if right:
            crosses = (self.z == NZ - 1).astype(jnp.int32)
            z = (self.z + 1) % NZ
        else:
            crosses = (self.z == 0).astype(jnp.int32)
            z = (self.z + NZ - 1) % NZ
        return self.at(z=z, h=(self.h + crosses) % 2)

    def others_z(self):
        return [((self.z + d) % NZ, self.at(z=(self.z + d) % NZ)) for d in range(1, NZ)]

    def others_y(self):
        return [self.at(y=(self.y + d) % self.ny) for d in range(1, self.ny)]

    def others_xc(self):
        found = []
        for d in range(1, 2 * self.nx):
            to_x, from_x = (self.x + d // 2) % self.nx, (self.x + self.nx - d // 2) % self.nx
            c = (self.c + d % 2) % 2
            found.append((to_x * 2 + c, from_x * 2 + c, self.at(x=to_x, c=c)))
        return found

    def opposite(self):
        return self.at(h=1 - self.h)


def greet(devices):
    barrier = pltpu.get_barrier_semaphore()
    for device in devices:
        pl.semaphore_signal(barrier, inc=1, device_id=device, device_id_type=MESH)


def await_greetings(count):
    pl.semaphore_wait(pltpu.get_barrier_semaphore(), count)


def near_mask(near, counts, width):
    blocks, listed = near.shape
    row = lax.broadcasted_iota(jnp.int32, (blocks, blocks), 0)
    own = row == lax.broadcasted_iota(jnp.int32, (blocks, blocks), 1)
    counts = jnp.sum(jnp.where(own, jnp.broadcast_to(counts, (blocks, blocks)), 0), axis=1, keepdims=True)
    lanes = lax.broadcasted_iota(jnp.int32, (blocks, width), 1)
    mask = jnp.zeros((blocks, width), F32)
    for n in range(listed):
        hit = jnp.where(near[:, n : n + 1] == lanes, 1.0, 0.0)
        mask = mask + jnp.where(counts > n, hit, 0.0)
    return mask


def pair_list(place, row_mask, col_mask):
    z, h, c, x, ny = place.z, place.h, place.c, place.x, place.ny
    sources_x = SOURCES_Y + ny
    rows, cols = row_mask.shape[0], col_mask.shape[0]
    own = rows + cols
    lane = lax.broadcasted_iota(jnp.int32, (128, 128), 0)
    k = lax.broadcasted_iota(jnp.int32, (128, 128), 1)
    from_row = (k // 4) * (NZ * 4) + z * 4 + k % 4
    from_col = x * 16 + (k // 4 + h) % 2 * 8 + c * 4 + k % 4
    bf = jnp.bfloat16
    pick_row = jnp.where((lane == from_row) & (k < ny * 4), 1.0, 0.0).astype(bf)
    pick_col = jnp.where((lane == from_col) & (k < 8), 1.0, 0.0).astype(bf)
    dot = functools.partial(jnp.dot, preferred_element_type=F32)
    live = jnp.concatenate([dot(row_mask.astype(bf), pick_row), dot(col_mask.astype(bf), pick_col)], axis=0)
    before = dot(live.astype(bf), jnp.where(lane < k, 1.0, 0.0).astype(bf))
    totals = jnp.broadcast_to(jnp.sum(live, axis=1, keepdims=True), (own, 128))
    one = lax.broadcasted_iota(jnp.int32, (own, own), 0)
    other = lax.broadcasted_iota(jnp.int32, (own, own), 1)
    above = (one > other) & ((one < rows) | (other >= rows))
    offset = dot(jnp.where(above, 1.0, 0.0).astype(bf), totals.astype(bf))
    first = jnp.where(lax.broadcasted_iota(jnp.int32, (own, 128), 0) < rows, 0.0, 128.0 * COLS_AT)
    rank = jnp.where(live > 0.5, before + offset + first, -1.0)

    a = lax.broadcasted_iota(jnp.int32, (own, 128), 0)
    k = lax.broadcasted_iota(jnp.int32, (own, 128), 1)
    unit = jnp.where(k // 4 == 0, z, AHEAD + z % HALF)
    is_row = a < rows
    own_block = jnp.where(is_row, a, a - rows + sources_x * 4)
    far_block = jnp.where(is_row, SOURCES_Y * 4 + k, unit * 4 + k % 4)
    far_slot = jnp.where(is_row, k, ny * 4 + k)
    code = (own_block + 128 * far_block + 16384 * far_slot).astype(F32)

    fill = jnp.zeros((128 - own, 128), F32)
    rank_t = jnp.transpose(jnp.concatenate([rank, fill - 1.0], axis=0))[:16]
    code_t = jnp.transpose(jnp.concatenate([code, fill], axis=0))[:16]
    slots = lax.broadcasted_iota(jnp.int32, (16, 128), 1).astype(F32)
    packed = [jnp.zeros((16, 128), F32) for _ in range(MAX_PAIRS_ROWS)]
    for one in range(own):
        rank_one = jnp.broadcast_to(rank_t[:, one : one + 1], (16, 128))
        code_one = jnp.broadcast_to(code_t[:, one : one + 1], (16, 128))
        for r in range(MAX_PAIRS_ROWS):
            packed[r] = packed[r] + jnp.where(rank_one == slots + 128.0 * r, code_one, 0.0)
    listing = [jnp.sum(part, axis=0, keepdims=True) for part in packed]
    counts = [jnp.sum(part, axis=0, keepdims=True) for part in (totals[:rows], totals[rows:])]
    return jnp.concatenate(listing + counts, axis=0).astype(jnp.int32)


def gather_kernel(
    nx,
    ny,
    source_ref,
    adjoint_ref,
    points_hbm,
    near_rows_hbm,
    counts_rows_hbm,
    near_cols_hbm,
    counts_cols_hbm,
    blocks_ref,
    own_axes_ref,
    far_axes_ref,
    list_ref,
    points_ref,
    near_rows_ref,
    counts_rows_ref,
    near_cols_ref,
    counts_cols_ref,
    own_meta,
    meta_ref,
    through_send,
    through_recv,
    extra_send,
    extra_recv,
    y_send,
    y_recv,
    x_send,
    x_recv,
    meta_send,
    meta_recv,
    local_sem,
    small_sem,
):
    smalls = [
        pltpu.make_async_copy(src, dst, small_sem.at[i])
        for i, (src, dst) in enumerate(
            (
                (points_hbm, points_ref),
                (near_rows_hbm, near_rows_ref),
                (counts_rows_hbm, counts_rows_ref),
                (near_cols_hbm, near_cols_ref),
                (counts_cols_hbm, counts_cols_ref),
            )
        )
    ]
    for copy in smalls:
        copy.start()
    place = Place(nx, ny)
    z, x, y = place.z, place.x, place.y
    per_device = source_ref.shape[0]
    sources_x = SOURCES_Y + ny
    right, left = place.beside(True), place.beside(False)
    sides = (right, left)
    others_z, others_y, others_xc = place.others_z(), place.others_y(), place.others_xc()
    opposite = place.opposite()
    met = [device for _, device in others_z] + others_y + [device for _, _, device in others_xc]
    met = met + [opposite]
    crosses = (z == 0) | (z == NZ - 1)
    over = place.at(z=NZ - 1 - z, h=1 - place.h)
    greet(met)

    @pl.when(crosses)
    def _():
        greet([over])

    for copy in smalls:
        copy.wait()
    points = points_ref[...].astype(F32).reshape(3 * per_device, 128)
    row_mask = near_mask(near_rows_ref[...], counts_rows_ref[...], 128)
    col_mask = near_mask(near_cols_ref[...], counts_cols_ref[...], 128)
    for which, mask in enumerate((row_mask, col_mask)):
        own_meta[which] = jnp.concatenate([points, mask], axis=0).astype(jnp.bfloat16)

    await_greetings(len(met) + crosses.astype(jnp.int32))

    def remote(src, dst, send, recv, device):
        return pltpu.make_async_remote_copy(
            src_ref=src, dst_ref=dst, send_sem=send, recv_sem=recv, device_id=device, device_id_type=MESH
        )

    chunks = per_device * SPLIT
    depth = source_ref.shape[1] // SPLIT
    hop = 3 * chunks // 4

    def part(ref, s):
        return ref.at[s // SPLIT, pl.ds(s % SPLIT * depth, depth)]

    def mirrored(side):
        return z if side == 0 else NZ - 1 - z

    def slot_of(side, unit):
        return unit if side == 0 else NZ - 1 - unit

    def through_unit(side, m, t):
        near = jnp.where(m < HALF, m - 1 - t, HALF - 1 - t)
        ahead = HALF - 1 - (t - m)
        is_near = (m >= HALF) | (t < m)
        return jnp.where(is_near, slot_of(side, near), AHEAD + (ahead if side == 0 else HALF - 1 - ahead))

    def passes_on(m, t):
        return (m >= HALF) | (t < HALF - 1)

    def through_copy(side, t, b):
        m = mirrored(side)
        unit = through_unit(side, m, t)
        crossed = AHEAD + unit if side == 0 else AHEAD + unit - HALF
        return remote(
            part(blocks_ref.at[unit], b),
            part(blocks_ref.at[jnp.where(m == NZ - 1, crossed, unit)], b),
            through_send.at[side, t + 1],
            through_recv.at[side, jnp.where(m < HALF, t + 1, t), b],
            sides[side],
        )

    def through_arrival(side, t, b):
        slot = part(blocks_ref.at[through_unit(side, mirrored(side), t)], b)
        return remote(slot, slot, through_send.at[side, t + 1], through_recv.at[side, t, b], sides[side])

    def extra_copy(side, e, b):
        slot = part(blocks_ref.at[slot_of(side, mirrored(side) - 1 - e)], b)
        return remote(slot, slot, extra_send.at[side, e + 1], extra_recv.at[side, e + 1, b], sides[side])

    def extra_arrival(side, e, b):
        slot = part(blocks_ref.at[slot_of(side, mirrored(side) - 1 - e)], b)
        return remote(slot, slot, extra_send.at[side, e + 1], extra_recv.at[side, e, b], sides[side])

    def own_copy(side, b):
        send, recv = through_send.at[side, 0], through_recv.at[side, 0, b]
        return remote(part(adjoint_ref, b), part(blocks_ref.at[z], b), send, recv, sides[side])

    def own_extra_copy(side, b):
        send, recv = extra_send.at[side, 0], extra_recv.at[side, 0, b]
        return remote(part(adjoint_ref, b), part(blocks_ref.at[z], b), send, recv, sides[side])

    def sends_extra(m):
        return (m >= HALF) & (m < NZ - 1)

    metas = []
    mine = x * 2 + place.c
    first_y = NZ + 2 * nx
    own_slots = [z, NZ + mine, first_y + y, first_y + ny]
    for d, (_, device) in enumerate(others_z):
        metas.append((0, own_slots[0], d, device, (z + NZ - 1 - d) % NZ))
    for d, (_, source, device) in enumerate(others_xc):
        metas.append((1, own_slots[1], NZ + d, device, NZ + source))
    for d, device in enumerate(others_y):
        metas.append((1, own_slots[2], first_y + d, device, first_y + (y + ny - 1 - d) % ny))
    metas.append((1, first_y + ny + 1, first_y + ny, opposite, first_y + ny + 1))
    meta_out = [
        remote(own_meta.at[which], meta_ref.at[slot], meta_send.at[s], meta_recv.at[s], device)
        for which, slot, s, device, _ in metas
    ]
    meta_in = [
        remote(own_meta.at[which], meta_ref.at[slot], meta_send.at[s], meta_recv.at[s], device)
        for which, _, s, device, slot in metas
    ]
    for copy in meta_out:
        copy.start()
    for b in range(chunks):
        for side in (0, 1):
            m = mirrored(side)

            @pl.when(m < HALF)
            def _():
                own_copy(side, b).start()

            @pl.when(sends_extra(m) & ((m > HALF) | (b < hop)))
            def _():
                own_extra_copy(side, b).start()

    y_out, y_in, x_out, x_in = [], [], [], []
    for d, device in enumerate(others_y):
        sems = (y_send.at[d], y_recv.at[d], device)
        y_out.append(remote(source_ref, blocks_ref.at[SOURCES_Y + y], *sems))
        y_in.append(remote(source_ref, blocks_ref.at[SOURCES_Y + (y + ny - 1 - d) % ny], *sems))
    for d, (_, source, device) in enumerate(others_xc):
        sems = (x_send.at[d], x_recv.at[d], device)
        x_out.append(remote(source_ref, blocks_ref.at[sources_x + mine], *sems))
        x_in.append(remote(source_ref, blocks_ref.at[sources_x + source], *sems))
    for copy in y_out + x_out:
        copy.start()
    locals_ = [
        pltpu.make_async_copy(adjoint_ref, blocks_ref.at[z], local_sem.at[0]),
        pltpu.make_async_copy(source_ref, blocks_ref.at[SOURCES_Y + y], local_sem.at[1]),
        pltpu.make_async_copy(source_ref, blocks_ref.at[sources_x + mine], local_sem.at[2]),
    ]
    for copy in locals_:
        copy.start()
    for which, slot in zip((0, 1, 1, 1), own_slots):
        meta_ref[slot] = own_meta[which]

    def ring_step(s, carry):
        for side in (0, 1):
            m = mirrored(side)
            far = s - hop * (m - HALF + 1)
            near = s - hop
            ahead = s - hop * (HALF + 1) + (chunks - hop) * m
            is_near = near < chunks * m
            q = jnp.where(m >= HALF, far, jnp.where(is_near, near, ahead))
            comes = (q >= 0) & (q < HALF * chunks) & ((m >= HALF) | is_near | (ahead >= chunks * m))
            t, b = jnp.maximum(q, 0) // chunks, jnp.maximum(q, 0) % chunks

            @pl.when(comes)
            def _():
                through_arrival(side, t, b).wait_recv()

                @pl.when(passes_on(m, t))
                def _():
                    through_copy(side, t, b).start()

            late = far - HALF * chunks
            is_late = (m > HALF) & (m < NZ - 1) & (late >= 0) & (late < chunks)
            is_early = (m == NZ - 2) & (near >= 0) & (near < chunks)

            @pl.when(is_late | is_early)
            def _():
                e = jnp.where(is_late & (m == NZ - 2), 1, 0)
                b = jnp.where(is_late, late, near)
                extra_arrival(side, e, b).wait_recv()
                extra_copy(side, e, b).start()

            @pl.when((m == HALF) & (late == 0))
            def _():
                for b in range(hop, chunks):
                    own_extra_copy(side, b).start()

        return carry

    slots = (HALF + 1) * hop + HALF * chunks
    fars = far_axes_ref.shape[0]
    first_far = first_y
    each = -(-fars // (slots - MET_AT - 1))
    at_end = (z == 0) | (z == NZ - 1)
    listed_at = jnp.where(at_end, LISTED_AT[0], LISTED_AT[1])
    axis = lax.broadcasted_iota(jnp.int32, (4 * per_device, 3 * 128), 0)
    wanted = lax.broadcasted_iota(jnp.int32, (4 * per_device, 3 * 128), 1) // 128 * per_device

    def spread_far(j):
        spread = jnp.where(axis == wanted + j % per_device, 1.0, 0.0).astype(jnp.bfloat16)
        far_axes_ref[j] = lax.dot_general(
            meta_ref[first_far + j // per_device], spread, (((0,), (0,)), ((), ())), preferred_element_type=F32
        )

    def list_pairs():
        masks = [meta_ref[u].astype(F32)[3 * per_device :] for u in range(first_y)]
        row_masks = jnp.concatenate(masks[:NZ], axis=0)
        col_masks = jnp.concatenate(masks[NZ:], axis=0)
        list_ref[...] = pair_list(place, row_masks, col_masks)
        for u in range(first_y):
            tile = meta_ref[u].astype(F32)
            for b in range(per_device):
                for c in range(3):
                    row = c * per_device + b
                    own_axes_ref[u * per_device + b, c : c + 1, :] = tile[row : row + 1]

    def ring_and_more(s, carry):
        ring_step(s, carry)

        @pl.when(s == MET_AT)
        def _():
            for copy in meta_in:
                copy.wait_recv()

        @pl.when(s == listed_at)
        def _():
            list_pairs()

        for e in range(each):
            j = (s - MET_AT - 1) * each + e

            @pl.when((j >= 0) & (j < fars))
            def _():
                spread_far(j)

        return carry

    lax.fori_loop(hop, slots, ring_and_more, 0)

    for side in (0, 1):

        @pl.when(mirrored(side) == NZ - 1)
        def _():
            def kept(s, carry):
                extra_arrival(side, s // chunks, s % chunks).wait_recv()
                return carry

            lax.fori_loop(0, (HALF - 1) * chunks, kept, 0)


    for copy in y_in + x_in:
        copy.wait_recv()
    for copy in locals_:
        copy.wait()
    for copy in y_out + x_out + meta_out:
        copy.wait_send()
    def unit_sent(semaphore):
        remote(blocks_ref.at[z], blocks_ref.at[z], semaphore, through_recv.at[0, 0, 0], right).wait_send()

    for side in (0, 1):
        m = mirrored(side)

        @pl.when(m < HALF)
        def _():
            unit_sent(through_send.at[side, 0])

        @pl.when(sends_extra(m))
        def _():
            unit_sent(extra_send.at[side, 0])

        for t in range(HALF):

            @pl.when(passes_on(m, t))
            def _():
                unit_sent(through_send.at[side, t + 1])

        for e in range(2):

            @pl.when((m > HALF + e) & (m < NZ - 1))
            def _():
                unit_sent(extra_send.at[side, e + 1])


UNROLL = 8
STATIC_ROWS = 64
STATIC_COLS = 24


def decode(code, rows, shift):
    own_block = code & 127
    return own_block, (code >> 7) & 127, code >> 14, jnp.where(own_block < rows, own_block, own_block - shift)


def pair_term(blocks, own_axes_ref, far_axes, entry):
    own_block, far_block, far_slot, acc_slot = entry
    weights = lax.dot_general(
        blocks[far_block], blocks[own_block], (((1,), (1,)), ((), ())), preferred_element_type=F32
    )
    tile = own_axes_ref[acc_slot]
    own_axes = [jnp.broadcast_to(tile[c : c + 1], (8, 128)) for c in range(3)]
    sums = [jnp.zeros((8, 128), F32) for _ in range(3)]
    for r in range(16):
        at = slice(8 * r, 8 * r + 8)
        d = [far_axes[far_slot, at, 128 * c : 128 * c + 128] - own_axes[c] for c in range(3)]
        inverse = lax.rsqrt(d[0] * d[0] + d[1] * d[1] + d[2] * d[2] + EPS2)
        scaled = weights[at] * (inverse * inverse * inverse)
        sums = [sums[c] + d[c] * scaled for c in range(3)]
    return sums


def pair_kernel(rows, own, shift, list_ref, blocks, own_axes_ref, far_axes, out_ref, acc):
    per_device = out_ref.shape[1] // 4
    out_ref[...] = jnp.zeros_like(out_ref)
    kinds = []
    for kind, (first, done) in enumerate(((0, STATIC_ROWS), (COLS_AT, STATIC_COLS))):
        kinds.append((first, done, list_ref[MAX_PAIRS_ROWS + kind, 0]))

    @pl.when((kinds[0][2] > STATIC_ROWS) | (kinds[1][2] > STATIC_COLS))
    def _():
        acc[...] = jnp.zeros_like(acc)
        for first, done, count in kinds:

            def step(i, carry):
                for u in range(UNROLL):
                    k = i * UNROLL + u
                    entry = decode(list_ref[first + k // 128, k % 128], rows, shift)
                    sums = pair_term(blocks, own_axes_ref, far_axes, entry)
                    slot = jnp.where(k < count, entry[3], own)
                    for c in range(3):
                        acc[slot, c] = acc[slot, c] + sums[c]
                return carry

            lax.fori_loop(done // UNROLL, (count + UNROLL - 1) // UNROLL, step, 0)
        for a in range(own):
            for c in range(3):
                row = c * per_device + a % per_device
                out_ref[a // per_device, row : row + 1, :] = jnp.sum(acc[a, c], axis=0, keepdims=True)


def sums_kernel(
    nx,
    ny,
    rows,
    own,
    shift,
    list_ref,
    listing_ref,
    blocks,
    own_axes_ref,
    far_axes,
    rest_ref,
    out_ref,
    terms,
    parts_ref,
    landed,
    send_sem,
    recv_sem,
):
    place = Place(nx, ny)
    z, x = place.z, place.x
    others_z, others_xc = place.others_z(), place.others_xc()
    mine = x * 2 + place.c
    met = [device for _, device in others_z] + [device for _, _, device in others_xc]
    greet(met)
    per_device = out_ref.shape[1]

    terms[...] = jnp.zeros_like(terms)
    k = lax.broadcasted_iota(jnp.int32, (own, 128), 1)
    owner = lax.broadcasted_iota(jnp.int32, (own, 128), 0)

    def static_pairs(kind, first, length, units):
        def step(i, carry):
            done = []
            for u in range(UNROLL):
                entry = decode(list_ref[first, i * UNROLL + u], rows, shift)
                sums = pair_term(blocks, own_axes_ref, far_axes, entry)
                done.append(jnp.concatenate([jnp.sum(part, axis=0, keepdims=True) for part in sums], axis=1))
            terms[pl.ds(pl.multiple_of(i * UNROLL, UNROLL), UNROLL), :] = jnp.concatenate(done, axis=0)
            return carry

        lax.fori_loop(0, length // UNROLL, step, 0)
        codes = jnp.broadcast_to(listing_ref[first : first + 1, :], (own, 128))
        at = MAX_PAIRS_ROWS + kind
        count = jnp.broadcast_to(listing_ref[at : at + 1, :], (own, 128))
        has = (decode(codes, rows, shift)[3] == owner) & (k < count) & (k < length)
        owns = jnp.where(has, 1.0, 0.0)
        acc = jnp.dot(owns, terms[...], preferred_element_type=F32, precision=lax.Precision.HIGHEST)
        for u in units:
            for c in range(3):
                at = slice(c * per_device, (c + 1) * per_device)
                parts_ref[u, at, :] = (
                    rest_ref[u, at, :] + acc[u * per_device : (u + 1) * per_device, 128 * c : 128 * c + 128]
                )

    outgoing, incoming = [], []

    def both(s, theirs, mine, source, device):
        for slot, copies in ((mine, outgoing), (source, incoming)):
            copies.append(
                pltpu.make_async_remote_copy(
                    src_ref=parts_ref.at[theirs],
                    dst_ref=landed.at[slot],
                    send_sem=send_sem.at[s],
                    recv_sem=recv_sem.at[s],
                    device_id=device,
                    device_id_type=MESH,
                )
            )

    for d, (other, device) in enumerate(others_z):
        both(d, other, z, (z + NZ - 1 - d) % NZ, device)
    for d, (other, source, device) in enumerate(others_xc):
        both(NZ + d, NZ + other, NZ + mine, NZ + source, device)

    static_pairs(0, 0, STATIC_ROWS, range(NZ))
    await_greetings(len(met))
    for copy in outgoing[: NZ - 1][::-1]:
        copy.start()
    static_pairs(1, COLS_AT, STATIC_COLS, range(NZ, NZ + 2 * nx))
    for copy in outgoing[NZ - 1 :]:
        copy.start()
    landed[z] = parts_ref[z]
    landed[NZ + mine] = parts_ref[NZ + mine]
    for copy in incoming:
        copy.wait_recv()
    total = landed[0]
    for u in range(1, NZ + 2 * nx):
        total = total + landed[u]
    for c in range(3):
        out_ref[c] = total[c * per_device : (c + 1) * per_device]
    for copy in outgoing:
        copy.wait_send()


def shards(
    nx,
    ny,
    source_strength,
    adjoint_strength,
    node_points,
    near_rows,
    counts_rows,
    near_cols,
    counts_cols,
):
    _, per_device, size_block, conditions = source_strength.shape
    units = SOURCES_Y + ny + 2 * nx
    metas = NZ + 2 * nx + ny + 2
    dma = pltpu.SemaphoreType.DMA
    any_space = pl.BlockSpec(memory_space=pl.ANY)
    hbm = pl.BlockSpec(memory_space=pltpu.HBM)
    fars = (ny + 2) * per_device
    small = pltpu.CompilerParams(vmem_limit_bytes=8 * 1024 * 1024)
    vmem = pl.BlockSpec(memory_space=pltpu.VMEM)
    blocks, own_axes, far_axes, listing = pl.pallas_call(
        functools.partial(gather_kernel, nx, ny),
        name="gather",
        out_shape=(
            jax.ShapeDtypeStruct((units, per_device, size_block, conditions), jnp.bfloat16),
            jax.ShapeDtypeStruct(((NZ + 2 * nx) * per_device, 8, 128), F32),
            jax.ShapeDtypeStruct((fars, size_block, 3 * 128), F32),
            jax.ShapeDtypeStruct((8, 128), jnp.int32),
        ),
        in_specs=[hbm] * 7,
        out_specs=(any_space, vmem, vmem, vmem),
        scratch_shapes=[
            pltpu.VMEM((3, per_device, size_block), jnp.bfloat16),
            pltpu.VMEM((per_device, near_rows.shape[2]), jnp.int32),
            pltpu.VMEM((1, per_device), jnp.int32),
            pltpu.VMEM((per_device, near_cols.shape[2]), jnp.int32),
            pltpu.VMEM((1, per_device), jnp.int32),
            pltpu.VMEM((2, 4 * per_device, 128), jnp.bfloat16),
            pltpu.VMEM((metas, 4 * per_device, 128), jnp.bfloat16),
            dma((2, HALF + 1)),
            dma((2, HALF, per_device * SPLIT)),
            dma((2, HALF)),
            dma((2, HALF, per_device * SPLIT)),
            dma((max(ny - 1, 1),)),
            dma((max(ny - 1, 1),)),
            dma((2 * nx - 1,)),
            dma((2 * nx - 1,)),
            dma((metas,)),
            dma((metas,)),
            dma((3,)),
            dma((5,)),
        ],
        compiler_params=pltpu.CompilerParams(
            collective_id=0, has_side_effects=True, vmem_limit_bytes=16 * 1024 * 1024
        ),
    )(
        *(
            pltpu.with_memory_space_constraint(operand, pltpu.HBM)
            for operand in (
                source_strength[0],
                adjoint_strength[0],
                jnp.transpose(node_points[0], (1, 0, 2)),
                near_rows[0],
                counts_rows,
                near_cols[0],
                counts_cols,
            )
        )
    )
    rows = NZ * per_device
    own = rows + 2 * nx * per_device
    shift = (SOURCES_Y + ny) * per_device - rows
    blocks = blocks.reshape(units * per_device, size_block, conditions)
    smem = pl.BlockSpec(memory_space=pltpu.SMEM)
    parts_shape = (NZ + 2 * nx, 4 * per_device, 128)
    rest = pl.pallas_call(
        functools.partial(pair_kernel, rows, own, shift),
        name="pairs",
        out_shape=jax.ShapeDtypeStruct(parts_shape, F32),
        in_specs=[smem, vmem, vmem, vmem],
        out_specs=vmem,
        scratch_shapes=[pltpu.VMEM((own + 1, 3, 8, 128), F32)],
        compiler_params=small,
    )(listing, blocks, own_axes, far_axes)
    total = pl.pallas_call(
        functools.partial(sums_kernel, nx, ny, rows, own, shift),
        name="sums",
        out_shape=jax.ShapeDtypeStruct((3, per_device, 128), F32),
        in_specs=[smem] + [vmem] * 5,
        out_specs=vmem,
        scratch_shapes=[
            pltpu.VMEM((128, 3 * 128), F32),
            pltpu.VMEM(parts_shape, F32),
            pltpu.VMEM(parts_shape, F32),
            dma((NZ + 2 * nx,)),
            dma((NZ + 2 * nx,)),
        ],
        compiler_params=pltpu.CompilerParams(
            collective_id=1, has_side_effects=True, vmem_limit_bytes=8 * 1024 * 1024
        ),
    )(listing, listing, blocks, own_axes, far_axes, rest)
    return jnp.transpose(total, (1, 0, 2))[None]


def solution(mesh):
    nx, ny = mesh.shape["blk"] // 4, mesh.shape["wide"] // NZ
    return jax.shard_map(
        functools.partial(shards, nx, ny),
        mesh=mesh,
        in_specs=(
            P("blk", "wide", None, None),
            P("blk", "wide", None, None),
            P("blk", "wide", None, None),
            P("blk", "wide", None),
            P("blk", "wide"),
            P("blk", "wide", None),
            P("blk", "wide"),
        ),
        out_specs=P("blk", "wide", None, None),
        check_vma=False,
    )
```
